32 devices in a mesh: section: 2 (over x), blk: 16 (over z, y, core).
Axes of the slice: x: 2, y: 2, z: 4, core: 2. Of those that a mesh axis runs over, the one named last changes fastest.
Arguments:
- raw_traces: bfloat16 [128, 8192], P('blk', 'section'), may hold values from -6 to 6
- valid_mask: int32 [128, 8], P('blk', 'section'), may hold values from 0 to 1, as said below
- block_order: int32 [16], replicated, may hold values from 0 to 15, each once
Outputs:
- correlations: float32 [16, 128, 256], P('section', 'blk')
The draws below stay inside these ranges and needn't reach their ends.
Inputs may be any that keep to these rules, and one draw needn't show every extreme that they name: `valid_mask`: a station either has no valid segment at all, or each of its segments is valid independently. `block_order`: each block index once.
All inputs are finite; a program needn't handle non-finite values.
Results may differ from the reference program's by a relative error of at most 0.0063.
Values may be sent and summed in bfloat16 or wider, within the bound.
No kernel may reach another device: no remote copies, remote signals or barrier semaphores. Data moves between devices by JAX's collectives and lax.ppermute only.
A program may use at most 64 MiB of HBM per device.

```python
import math
import jax
import jax.numpy as jnp
from jax import lax

ST_DEV = 8
L = 1024
NF = 384
BIN_LO = 8
LAGS = 256
TAPS = 33
HW = 50
WF = 32
STEPS = 2
STATIONS = 128
SEGS = 8
SAMPLES = 8192
NS = 16
RIM = 66
N_BLK = 16


def draw_valid_mask(key, part):
    dead_key = jax.random.fold_in(key, 11)
    each_key = jax.random.fold_in(key, 23)
    alive = jax.random.randint(dead_key, (STATIONS, 1), 0, 16) != 0
    valid = jax.random.randint(each_key, (STATIONS, SEGS), 0, 8) != 0
    return (alive & valid).astype(jnp.int32)


def level_of(own_key, dims, shards, smallest, largest):
    loudness, own = 1.0, jax.random.fold_in(own_key, 6)
    for position, blocks in shards:
        draws = jnp.exp(jax.random.uniform(jax.random.fold_in(own, position), (blocks,), jnp.float32, smallest / len(shards), largest / len(shards)))
        loudness = loudness * jnp.repeat(draws, dims[position] // blocks).reshape([-1 if axis == position else 1 for axis in range(len(dims))])
    return loudness


def normal_values(own_key, extent, scale, most, split=(), kind=jnp.bfloat16):
    entries = jax.random.normal(own_key, extent, jnp.float32) * scale
    if len(split) > 0:
        entries = level_of(own_key, extent, split, -0.22, 0.18) * entries
    return jnp.clip(entries, min=-most, max=most).astype(kind)


def setup_inputs(seed: int = 0) -> dict:
    seeds = jax.random.split(jax.random.key(seed), 4)
    raw_traces = normal_values(seeds[0], (STATIONS, SAMPLES), 1.0, 6.0, ((0, 16), (1, 2)))
    valid_mask = draw_valid_mask(jax.random.fold_in(seeds[3], 71), 0)
    block_order = jax.random.permutation(seeds[2], N_BLK).astype(jnp.int32)
    return {"raw_traces": raw_traces, "valid_mask": valid_mask, "block_order": block_order}


def bandpass_taps():
    offsets = jnp.arange(TAPS, dtype=jnp.float32) - (TAPS - 1) // 2
    low = BIN_LO / L
    high = (BIN_LO + NF) / L
    window = 0.5 + 0.5 * jnp.cos(2.0 * math.pi * offsets / (TAPS + 1))
    return window * (2.0 * high * jnp.sinc(2.0 * high * offsets) - 2.0 * low * jnp.sinc(2.0 * low * offsets))

def filter_normalize(padded):
    taps = bandpass_taps()
    width = padded.shape[1] - (TAPS - 1)
    filtered = taps[0] * padded[:, 0:width]
    for offset in range(1, TAPS):
        filtered = filtered + taps[offset] * padded[:, offset:offset + width]
    magnitude = jnp.abs(filtered)
    window_sum = lax.reduce_window(magnitude, jnp.zeros((), magnitude.dtype), lax.add, (1, 2 * HW + 1), (1, 1), 'VALID')
    centre = filtered[:, HW:HW + window_sum.shape[1]]
    return (centre / (window_sum / (2 * HW + 1) + 1e-06)).astype(jnp.bfloat16)

def forward_table():
    times = jnp.arange(L, dtype=jnp.int32)[:, None]
    bins = BIN_LO + jnp.arange(NF, dtype=jnp.int32)[None, :]
    phase = jnp.mod(times * bins, L).astype(jnp.float32) * (2.0 * math.pi / L)
    return jnp.concatenate([jnp.cos(phase), -jnp.sin(phase)], axis=1).astype(jnp.bfloat16)

def lag_table():
    bins = BIN_LO + jnp.arange(NF, dtype=jnp.int32)[:, None]
    shifts = jnp.arange(LAGS, dtype=jnp.int32)[None, :] - LAGS // 2
    phase = jnp.mod(bins * shifts, L).astype(jnp.float32) * (2.0 * math.pi / L)
    scale = 1.0 / math.sqrt(NF)
    return jnp.concatenate([jnp.cos(phase) * scale, -jnp.sin(phase) * scale], axis=0)

def whiten(normalized, maskvals):
    stations = normalized.shape[0]
    framed = normalized.reshape(-1, L)
    spectra = jnp.dot(framed, forward_table(), preferred_element_type=jnp.float32)
    spectra = spectra.reshape(stations, -1, 2 * NF)
    real_part = spectra[:, :, :NF]
    imag_part = spectra[:, :, NF:]
    amplitude = jnp.sqrt(real_part * real_part + imag_part * imag_part)
    smooth = lax.reduce_window(amplitude, jnp.zeros((), amplitude.dtype), lax.add, (1, 1, 2 * WF + 1), (1, 1, 1), ((0, 0), (0, 0), (WF, WF)))
    factor = maskvals[:, :, None] / (smooth / (2 * WF + 1) + 1e-06)
    return jnp.concatenate([real_part * factor, imag_part * factor], axis=2).astype(jnp.bfloat16)

def cross_lags(sources, receivers):
    source_real = sources[:, :, :NF].astype(jnp.float32)
    source_imag = sources[:, :, NF:].astype(jnp.float32)
    recv_real = receivers[:, :, :NF].astype(jnp.float32)
    recv_imag = receivers[:, :, NF:].astype(jnp.float32)
    real_sum = jnp.einsum('jsf,isf->jif', source_real, recv_real) + jnp.einsum('jsf,isf->jif', source_imag, recv_imag)
    imag_sum = jnp.einsum('jsf,isf->jif', source_real, recv_imag) - jnp.einsum('jsf,isf->jif', source_imag, recv_real)
    stacked = jnp.concatenate([real_sum, imag_sum], axis=2)
    count_src, count_rec = (stacked.shape[0], stacked.shape[1])
    lagged = jnp.dot(stacked.reshape(count_src * count_rec, 2 * NF), lag_table(), precision=lax.Precision.HIGHEST)
    return lagged.reshape(count_src, count_rec, LAGS)

def reference(raw_traces, valid_mask, block_order):
    padded = jnp.pad(raw_traces.astype(jnp.float32), ((0, 0), (RIM, RIM)))
    normalized = filter_normalize(padded)
    maskvals = valid_mask.astype(jnp.float32)
    whitened = whiten(normalized, maskvals)

    def one_block(owner):
        start = (owner * ST_DEV).astype(jnp.int32)
        sources = lax.dynamic_slice_in_dim(whitened, start, ST_DEV, 0)
        source_mask = lax.dynamic_slice_in_dim(maskvals, start, ST_DEV, 0)
        counts = jnp.dot(source_mask, maskvals.T, precision=lax.Precision.HIGHEST)
        return cross_lags(sources, whitened) / jnp.maximum(counts, 1.0)[:, :, None]
    blocks = lax.map(one_block, block_order[:STEPS])
    return blocks.reshape(NS, STATIONS, LAGS)
```

```python
import math

import jax
import jax.numpy as jnp
import numpy as np
from jax import lax
from jax.experimental import pallas as pl
from jax.experimental.pallas import tpu as pltpu
from jax.sharding import PartitionSpec as P

L = 1024
NF = 384
BIN_LO = 8
LAGS = 256
TAPS = 33
HW = 50
WF = 32
ST = 8
SEGS = 8
BLK = 256
ROWS = SEGS * L // BLK
PAD = 128

F32 = jnp.float32
BF16 = jnp.bfloat16


def halves(table):
    high = table.astype(BF16)
    low = (table - high.astype(np.float64)).astype(BF16)
    return high, low


def filter_table():
    k = np.arange(TAPS, dtype=np.float64) - (TAPS - 1) // 2
    low, high = BIN_LO / L, (BIN_LO + NF) / L
    window = 0.5 + 0.5 * np.cos(2.0 * math.pi * k / (TAPS + 1))
    taps = window * (2 * high * np.sinc(2 * high * k) - 2 * low * np.sinc(2 * low * k))
    shift = BLK // 2 + np.arange(BLK)[None, :] - np.arange(2 * BLK)[:, None] + (TAPS - 1) // 2
    inside = (shift >= 0) & (shift < TAPS)
    table = np.where(inside, taps[np.clip(shift, 0, TAPS - 1)], 0.0)
    return np.concatenate(halves(table), axis=1)


def mean_table():
    shift = BLK // 2 + np.arange(BLK)[None, :] - np.arange(2 * BLK)[:, None]
    return (np.abs(shift) <= HW).astype(BF16)


def smooth_table():
    bins = np.arange(NF)
    return (np.abs(bins[:, None] - bins[None, :]) <= WF).astype(BF16)


def forward_table():
    phase = np.mod(np.arange(L)[:, None] * (BIN_LO + np.arange(NF))[None, :], L) * (2.0 * math.pi / L)
    return np.concatenate([np.cos(phase), -np.sin(phase)], axis=1).astype(BF16)


def lag_table():
    shifts = np.arange(LAGS)[None, :] - LAGS // 2
    phase = np.mod((BIN_LO + np.arange(NF))[:, None] * shifts, L) * (2.0 * math.pi / L)
    table = np.concatenate([np.cos(phase), -np.sin(phase)], axis=0) / math.sqrt(NF)
    return halves(table)


def dot(a, b):
    return jnp.dot(a, b, preferred_element_type=F32)


def split(a):
    high = a.astype(BF16)
    return high, (a - high.astype(F32)).astype(BF16)


def spread(parts):
    half = parts[0].shape[1] - PAD
    rows = []
    for part in parts:
        rows += [part[:, i * BLK : (i + 1) * BLK].astype(F32) for i in range(half // BLK)]
    return rows


def mask_columns(parts):
    half = parts[0].shape[1] - PAD
    per = half // L
    tiles = [part[:, half:].astype(F32) for part in parts]
    column = jnp.concatenate([tile[:, g : g + 1] for tile in tiles for g in range(per)], axis=0)
    return tiles, column


def whitened_blocks(blocks, columns, taps, mean, table, smooth):
    count = len(blocks)
    zero = jnp.zeros((ST, BLK), F32)
    x = jnp.concatenate([t for rows in blocks for t in [zero, zero, *rows, zero, zero]], axis=0)
    n = x.shape[0]
    half = BLK // 2
    window = jnp.concatenate(
        [x[: n - 2 * ST, half:], x[ST : n - ST], x[2 * ST :, :half]], axis=1
    ).astype(BF16)
    both = dot(window, taps)
    filtered = both[:, :BLK] + both[:, BLK:]
    m = filtered.shape[0]
    size = jnp.abs(filtered)
    window = jnp.concatenate(
        [size[: m - 2 * ST, half:], size[ST : m - ST], size[2 * ST :, :half]], axis=1
    )
    high, low = split(window)
    total = dot(high, mean) + dot(low, mean)
    normal = filtered[ST : m - ST] / (total * (1.0 / (2 * HW + 1)) + 1e-06)
    span = (ROWS + 4) * ST
    per = L // BLK
    framed = []
    for b in range(count):
        part = normal[b * span : b * span + ROWS * ST].reshape(SEGS, per, ST, BLK)
        framed.append(
            jnp.concatenate([part[:, q].reshape(SEGS * ST, BLK) for q in range(per)], axis=1)
        )
    framed = jnp.concatenate(framed, axis=0).astype(BF16)
    spectra = dot(framed, table)
    real, imag = spectra[:, :NF], spectra[:, NF:]
    amplitude = jnp.sqrt(real * real + imag * imag)
    high, low = split(amplitude)
    smoothed = dot(high, smooth) + dot(low, smooth)
    factor = jnp.concatenate(columns, axis=0) / (smoothed * (1.0 / (2 * WF + 1)) + 1e-06)
    return jnp.concatenate([real * factor, imag * factor], axis=1).astype(BF16).astype(F32)


def kernel(own0, own1, src0, src1, taps, mean, table, smooth, lag_high, lag_low, out):
    own, src = (own0[...], own1[...]), (src0[...], src1[...])
    own_masks, own_column = mask_columns(own)
    src_masks, src_column = mask_columns(src)
    white = whitened_blocks(
        [spread(own), spread(src)], [own_column, src_column], taps[...], mean[...], table[...], smooth[...]
    )
    size = SEGS * ST
    recv, sent = white[:size], white[size:]
    rows, counts = [], []
    for n in range(ST):
        real = jnp.zeros((ST, NF), F32)
        imag = jnp.zeros((ST, NF), F32)
        for g in range(SEGS):
            line = sent[g * ST + n : g * ST + n + 1]
            tile = recv[g * ST : (g + 1) * ST]
            sr, si = line[:, :NF], line[:, NF:]
            rr, ri = tile[:, :NF], tile[:, NF:]
            real += rr * sr + ri * si
            imag += ri * sr - rr * si
        rows.append(jnp.concatenate([real, imag], axis=1))
        common = sum(s[n : n + 1] * r for s, r in zip(src_masks, own_masks))
        counts.append(jnp.sum(common, axis=1, keepdims=True))
    high, low = split(jnp.concatenate(rows, axis=0))
    both = dot(jnp.concatenate([high, low], axis=0), lag_high[...])
    lagged = both[:size] + both[size:] + dot(high, lag_low[...])
    lagged = lagged / jnp.maximum(jnp.concatenate(counts, axis=0), 1.0)
    out[...] = lagged.reshape(ST, ST, LAGS)


def correlate(own, src):
    tables = [filter_table(), mean_table(), forward_table(), smooth_table(), *lag_table()]
    return pl.pallas_call(
        kernel,
        out_shape=jax.ShapeDtypeStruct((ST, ST, LAGS), F32),
        in_specs=[pl.BlockSpec(memory_space=pltpu.VMEM)] * (4 + len(tables)),
        out_specs=pl.BlockSpec(memory_space=pltpu.VMEM),
        compiler_params=pltpu.CompilerParams(vmem_limit_bytes=32 * 1024 * 1024),
    )(*own, *src, *[jnp.asarray(t) for t in tables])


def shards(raw_traces, valid_mask, block_order):
    section = lax.axis_index("section")
    blocks = lax.axis_size("blk")
    me = lax.axis_index("blk")
    root = block_order[section]
    mask = jnp.pad(valid_mask.astype(BF16), ((0, 0), (0, PAD - valid_mask.shape[1])))
    mine = jnp.concatenate([raw_traces, mask], axis=1)
    other = lax.ppermute(mine, "section", [(0, 1), (1, 0)])
    own = (jnp.where(section == 0, mine, other), jnp.where(section == 0, other, mine))
    held = jnp.concatenate(own, axis=1)
    step = 1
    while step < blocks:
        got = lax.ppermute(held, "blk", [(i, i ^ step) for i in range(blocks)])
        held = jnp.where((me ^ root) & step == 0, held, got)
        step *= 2
    src = jnp.split(held, 2, axis=1)
    return correlate(own, src)


def solution(mesh):
    return jax.shard_map(
        shards,
        mesh=mesh,
        in_specs=(P("blk", "section"), P("blk", "section"), P()),
        out_specs=P("section", "blk", None),
        check_vma=False,
    )
```

```python
import math

import jax
import jax.numpy as jnp
import numpy as np
from jax import lax
from jax.experimental import pallas as pl
from jax.experimental.pallas import tpu as pltpu
from jax.sharding import PartitionSpec as P

L = 1024
NF = 384
BIN_LO = 8
LAGS = 256
TAPS = 33
HW = 50
WF = 32
ST = 8
SEGS = 8
BLK = 256
ROWS = SEGS * L // BLK
PAD = 128
LANES = 128

F32 = jnp.float32
BF16 = jnp.bfloat16


def halves(table):
    high = table.astype(BF16)
    low = (table - high.astype(np.float64)).astype(BF16)
    return high, low


def filter_table():
    k = np.arange(TAPS, dtype=np.float64) - (TAPS - 1) // 2
    low, high = BIN_LO / L, (BIN_LO + NF) / L
    window = 0.5 + 0.5 * np.cos(2.0 * math.pi * k / (TAPS + 1))
    taps = window * (2 * high * np.sinc(2 * high * k) - 2 * low * np.sinc(2 * low * k))
    shift = BLK // 2 + np.arange(BLK)[None, :] - np.arange(2 * BLK)[:, None] + (TAPS - 1) // 2
    inside = (shift >= 0) & (shift < TAPS)
    table = np.where(inside, taps[np.clip(shift, 0, TAPS - 1)], 0.0)
    return np.concatenate(halves(table), axis=1)


def mean_table():
    shift = BLK // 2 + np.arange(BLK)[None, :] - np.arange(2 * BLK)[:, None]
    return (np.abs(shift) <= HW).astype(BF16)


def smooth_table():
    bins = np.arange(NF)
    return (np.abs(bins[:, None] - bins[None, :]) <= WF).astype(BF16)


def forward_table():
    phase = np.mod(np.arange(L)[:, None] * (BIN_LO + np.arange(NF))[None, :], L) * (2.0 * math.pi / L)
    return np.concatenate([np.cos(phase), -np.sin(phase)], axis=1).astype(BF16)


def lag_table():
    shifts = np.arange(LAGS)[None, :] - LAGS // 2
    phase = np.mod((BIN_LO + np.arange(NF))[:, None] * shifts, L) * (2.0 * math.pi / L)
    table = np.concatenate([np.cos(phase), -np.sin(phase)], axis=0) / math.sqrt(NF)
    return halves(table)


def dot(a, b):
    return jnp.dot(a, b, preferred_element_type=F32)


def split(a):
    high = a.astype(BF16)
    return high, (a - high.astype(F32)).astype(BF16)


def spread(parts):
    rows = []
    for part in parts:
        half = part.shape[1] - PAD
        rows += [part[:, i * BLK : (i + 1) * BLK].astype(F32) for i in range(half // BLK)]
    return rows


def mask_rows(parts):
    per = (parts[0].shape[1] - PAD) // L
    return jnp.concatenate([p[:, p.shape[1] - PAD :].astype(F32)[:per] for p in parts], axis=0)


def mask_column(mask):
    diagonal = lax.broadcasted_iota(jnp.int32, (ST, LANES), 0) == lax.broadcasted_iota(
        jnp.int32, (ST, LANES), 1
    )
    tiles = [jnp.where(diagonal, mask[g : g + 1], 0.0) for g in range(SEGS)]
    return jnp.sum(jnp.concatenate(tiles, axis=0), axis=1, keepdims=True)


def whitened(parts, column, table):
    zero = jnp.zeros((2 * ST, BLK), F32)
    x = jnp.concatenate([zero, *spread(parts), zero], axis=0)
    n = x.shape[0]
    half = BLK // 2
    window = jnp.concatenate(
        [x[: n - 2 * ST, half:], x[ST : n - ST], x[2 * ST :, :half]], axis=1
    ).astype(BF16)
    both = dot(window, table(0))
    filtered = both[:, :BLK] + both[:, BLK:]
    m = filtered.shape[0]
    size = jnp.abs(filtered)
    window = jnp.concatenate(
        [size[: m - 2 * ST, half:], size[ST : m - ST], size[2 * ST :, :half]], axis=1
    )
    high, low = split(window)
    mean = table(1)
    total = dot(high, mean) + dot(low, mean)
    normal = filtered[ST : m - ST] / (total * (1.0 / (2 * HW + 1)) + 1e-06)
    per = L // BLK
    normal = normal.reshape(SEGS, per, ST, BLK)
    framed = jnp.concatenate([normal[:, q].reshape(SEGS * ST, BLK) for q in range(per)], axis=1)
    spectra = dot(framed.astype(BF16), table(2))
    real, imag = spectra[:, :NF], spectra[:, NF:]
    amplitude = jnp.sqrt(real * real + imag * imag)
    high, low = split(amplitude)
    smooth = table(3)
    smoothed = dot(high, smooth) + dot(low, smooth)
    factor = column / (smoothed * (1.0 / (2 * WF + 1)) + 1e-06)
    return jnp.concatenate([real * factor, imag * factor], axis=1).astype(BF16)


def pack(raw, mask, order, mine, wanted, carried, order_here, mask_here, sems):
    half = raw.shape[1]
    away = (wanted, carried)
    copies = [
        pltpu.make_async_copy(order, order_here, sems.at[0]),
        pltpu.make_async_copy(mask, mask_here, sems.at[1]),
        pltpu.make_async_copy(raw, mine.at[:, pl.ds(0, half)], sems.at[2]),
    ]
    for copy in copies:
        copy.start()
    mine[:, half:] = jnp.zeros((ST, PAD), BF16)
    me = lax.axis_index("blk")
    copies[0].wait()
    for i, source in enumerate((lax.axis_index("section"), me & 1)):
        away[i][...] = jnp.full(away[i].shape, order_here[source] ^ me, jnp.int32)
    copies[1].wait()
    segs, stations = mask.shape
    mine[:segs, half : half + stations] = mask_here[...].astype(F32).astype(BF16)
    copies[2].wait()


def ordered(swap, one, two):
    one, two = one[...], two[...]
    return jnp.where(swap == 0, one, two), jnp.where(swap == 0, two, one)


def receivers(mine, other, *refs):
    tables, (white, masks, *held, sems) = refs[:6], refs[6:]
    copies = [pltpu.make_async_copy(t, h, sems.at[i]) for i, (t, h) in enumerate(zip(tables, held))]
    for copy in copies:
        copy.start()
    parts = ordered(lax.axis_index("section"), mine, other)
    column = mask_column(mask_rows(parts))
    masks[...] = jnp.broadcast_to(column, masks.shape)

    def table(i):
        copies[i].wait()
        return held[i][...]

    white[...] = whitened(parts, column, table)
    copies[4].wait()
    copies[5].wait()


def correlate(held, twin, white, masks, *refs):
    tables, out = refs[:-1], refs[-1]
    parts = ordered(lax.axis_index("blk") & 1, held, twin)
    sent_mask = mask_rows(parts)
    column = mask_column(sent_mask)
    sent = whitened(parts, column, lambda i: tables[i][...]).astype(F32)
    lag_high, lag_low = tables[4:]
    recv = white[...].astype(F32)
    size = SEGS * ST
    common = sum(masks[g * ST : (g + 1) * ST] * sent_mask[g : g + 1] for g in range(SEGS))
    rows, counts = [], []
    for n in range(ST):
        real = jnp.zeros((ST, NF), F32)
        imag = jnp.zeros((ST, NF), F32)
        for g in range(SEGS):
            line = sent[g * ST + n : g * ST + n + 1]
            tile = recv[g * ST : (g + 1) * ST]
            sr, si = line[:, :NF], line[:, NF:]
            rr, ri = tile[:, :NF], tile[:, NF:]
            real += rr * sr + ri * si
            imag += ri * sr - rr * si
        rows.append(jnp.concatenate([real, imag], axis=1))
        counts.append(common[:, n : n + 1])
    high, low = split(jnp.concatenate(rows, axis=0))
    both = dot(jnp.concatenate([high, low], axis=0), lag_high[...])
    lagged = both[:size] + both[size:] + dot(high, lag_low[...])
    lagged = lagged / jnp.maximum(jnp.concatenate(counts, axis=0), 1.0)
    out[...] = lagged.reshape(ST, ST, LAGS)


VMEM = pl.BlockSpec(memory_space=pltpu.VMEM)
HBM = pl.BlockSpec(memory_space=pltpu.HBM)


def call(body, out_shape, in_specs, arrays, scratch=(), flops=0):
    size = sum(a.size * a.dtype.itemsize for a in arrays)
    arrays = [
        pltpu.with_memory_space_constraint(a, pltpu.HBM) if spec is HBM else a
        for a, spec in zip(arrays, in_specs)
    ]
    return pl.pallas_call(
        body,
        out_shape=out_shape,
        in_specs=in_specs,
        out_specs=jax.tree.map(lambda _: VMEM, out_shape),
        scratch_shapes=scratch,
        cost_estimate=pl.CostEstimate(flops=flops, bytes_accessed=size, transcendentals=0),
        compiler_params=pltpu.CompilerParams(vmem_limit_bytes=16 * 1024 * 1024),
    )(*arrays)


def shaped(*shape, dtype=BF16):
    return jax.ShapeDtypeStruct(shape, dtype)


def exchange(x, flip, axis="blk"):
    devices = lax.axis_size(axis)
    return lax.ppermute(x, axis, [(i, i ^ flip) for i in range(devices)])


def crossing(x, bit):
    axes = ("section", "blk")
    blocks = lax.axis_size("blk")
    near, far = [], []
    for s in range(2):
        for b in range(blocks):
            here = s * blocks + b
            if s == b % 2:
                near.append((here, s * blocks + (b ^ bit)))
            else:
                there = (1 - s) * blocks
                near.append((here, there + (b ^ 1)))
                far.append((here, there + (b ^ 1 ^ bit)))
    return lax.ppermute(x, axes, near), lax.ppermute(x, axes, far)


def shards(raw_traces, valid_mask, block_order):
    section = lax.axis_index("section")
    blocks = lax.axis_size("blk")
    me = lax.axis_index("blk")
    core = me & 1
    half = raw_traces.shape[1]
    width = half + PAD
    mine, away_wanted, away_carried = call(
        pack,
        [shaped(ST, width)] + [shaped(ST, width, dtype=jnp.int32)] * 2,
        [HBM] * 3,
        [raw_traces, valid_mask.T, block_order],
        [
            pltpu.SMEM(block_order.shape, jnp.int32),
            pltpu.VMEM(valid_mask.shape[::-1], jnp.int32),
            pltpu.SemaphoreType.DMA((3,)),
        ],
    )

    twin = exchange(mine, 1)
    held = jnp.where(away_carried & 1 == 0, mine, twin)
    bits = [1 << i for i in range(1, blocks.bit_length() - 1)]
    last = bits.pop()
    other = None
    while bits:
        flips, bits = bits[:2], bits[2:]
        low, steps = flips[0], 1 << len(flips)
        got = [exchange(held, low * k) for k in range(1, steps)]
        if other is None:
            other = exchange(mine, 1, "section")
        rel = away_carried & (low * (steps - 1))
        for k in range(1, steps):
            held = jnp.where(rel == low * k, got[k - 1], held)
    tables = [filter_table(), mean_table(), forward_table(), smooth_table(), *lag_table()]
    tables = [jnp.asarray(t) for t in tables]
    held, other = lax.optimization_barrier((held, other))
    near, far = crossing(held, last)
    white, masks, *tables = call(
        receivers,
        [shaped(SEGS * ST, 2 * NF), shaped(SEGS * ST, LANES, dtype=F32)]
        + [shaped(*t.shape) for t in tables],
        [VMEM] * 2 + [HBM] * len(tables),
        [mine, other, *tables],
        [pltpu.SemaphoreType.DMA((len(tables),))],
        flops=10**9,
    )
    near, far, white, masks = lax.optimization_barrier((near, far, white, masks))
    same = away_wanted & last == 0
    held = jnp.where(core == section, jnp.where(same, held, near), jnp.where(same, near, far))
    twin = exchange(held, 1)
    return call(
        correlate,
        shaped(ST, ST, LAGS, dtype=F32),
        [VMEM] * 10,
        [held, twin, white, masks, *tables],
        flops=10**9,
    )


def solution(mesh):
    return jax.shard_map(
        shards,
        mesh=mesh,
        in_specs=(P("blk", "section"), P("blk", "section"), P()),
        out_specs=P("section", "blk", None),
        check_vma=False,
    )
```

```python
import math

import jax
import jax.numpy as jnp
import numpy as np
from jax import lax
from jax.experimental import pallas as pl
from jax.experimental.pallas import tpu as pltpu
from jax.sharding import PartitionSpec as P

L = 1024
NF = 384
BIN_LO = 8
LAGS = 256
TAPS = 33
HW = 50
WF = 32
ST = 8
SEGS = 8
BLK = 256
ROWS = SEGS * L // BLK
PAD = 128
LANES = 128

F32 = jnp.float32
BF16 = jnp.bfloat16


def halves(table):
    high = table.astype(BF16)
    low = (table - high.astype(np.float64)).astype(BF16)
    return high, low


def filter_table():
    k = np.arange(TAPS, dtype=np.float64) - (TAPS - 1) // 2
    low, high = BIN_LO / L, (BIN_LO + NF) / L
    window = 0.5 + 0.5 * np.cos(2.0 * math.pi * k / (TAPS + 1))
    taps = window * (2 * high * np.sinc(2 * high * k) - 2 * low * np.sinc(2 * low * k))
    shift = BLK // 2 + np.arange(BLK)[None, :] - np.arange(2 * BLK)[:, None] + (TAPS - 1) // 2
    inside = (shift >= 0) & (shift < TAPS)
    table = np.where(inside, taps[np.clip(shift, 0, TAPS - 1)], 0.0)
    return np.concatenate(halves(table), axis=1)


def mean_table():
    shift = BLK // 2 + np.arange(BLK)[None, :] - np.arange(2 * BLK)[:, None]
    return (np.abs(shift) <= HW).astype(BF16)


def smooth_table():
    bins = np.arange(NF)
    return (np.abs(bins[:, None] - bins[None, :]) <= WF).astype(BF16)


def forward_table():
    phase = np.mod(np.arange(BLK)[:, None] * (BIN_LO + np.arange(NF))[None, :], L) * (2.0 * math.pi / L)
    return np.concatenate([np.cos(phase), -np.sin(phase)], axis=1).astype(BF16)


def lag_table():
    shifts = np.arange(LAGS)[None, :] - LAGS // 2
    phase = np.mod((BIN_LO + np.arange(NF))[:, None] * shifts, L) * (2.0 * math.pi / L)
    table = np.concatenate([np.cos(phase), -np.sin(phase)], axis=0) / math.sqrt(NF)
    return halves(table)


def dot(a, b):
    return jnp.dot(a, b, preferred_element_type=F32)


def split(a):
    high = a.astype(BF16)
    return high, (a - high.astype(F32)).astype(BF16)


def spread(parts):
    rows = []
    for part in parts:
        half = part.shape[1] - PAD
        rows += [part[:, i * BLK : (i + 1) * BLK].astype(F32) for i in range(half // BLK)]
    return rows


def mask_rows(parts):
    per = (parts[0].shape[1] - PAD) // L
    return jnp.concatenate([p[:, p.shape[1] - PAD :].astype(F32)[:per] for p in parts], axis=0)


def mask_column(mask):
    diagonal = lax.broadcasted_iota(jnp.int32, (ST, LANES), 0) == lax.broadcasted_iota(
        jnp.int32, (ST, LANES), 1
    )
    tiles = [jnp.where(diagonal, mask[g : g + 1], 0.0) for g in range(SEGS)]
    return jnp.sum(jnp.concatenate(tiles, axis=0), axis=1, keepdims=True)


def quarters(parts):
    parts = parts.reshape(SEGS, L // BLK, ST, 2 * NF)
    q0, q1, q2, q3 = (parts[:, q].reshape(SEGS * ST, 2 * NF) for q in range(L // BLK))
    turn = (BIN_LO + lax.broadcasted_iota(jnp.int32, (1, 2 * NF), 1)) % 4
    even = turn % 2 == 0
    here = jnp.where(even, q0 + q2, q0 - q2)
    there = jnp.where(even, q1 + q3, q1 - q3)
    there = jnp.where(turn >= 2, -there, there)
    real, imag = there[:, :NF], there[:, NF:]
    even = even[:, :NF]
    return here[:, :NF] + jnp.where(even, real, imag), here[:, NF:] + jnp.where(even, imag, -real)


def whitened(parts, column, table):
    zero = jnp.zeros((2 * ST, BLK), F32)
    x = jnp.concatenate([zero, *spread(parts), zero], axis=0)
    n = x.shape[0]
    half = BLK // 2
    window = jnp.concatenate(
        [x[: n - 2 * ST, half:], x[ST : n - ST], x[2 * ST :, :half]], axis=1
    ).astype(BF16)
    both = dot(window, table(0))
    filtered = both[:, :BLK] + both[:, BLK:]
    m = filtered.shape[0]
    size = jnp.abs(filtered)
    window = jnp.concatenate(
        [size[: m - 2 * ST, half:], size[ST : m - ST], size[2 * ST :, :half]], axis=1
    )
    high, low = split(window)
    mean = table(1)
    total = dot(high, mean) + dot(low, mean)
    normal = filtered[ST : m - ST] / (total * (1.0 / (2 * HW + 1)) + 1e-06)
    real, imag = quarters(dot(normal.astype(BF16), table(2)))
    amplitude = jnp.sqrt(real * real + imag * imag)
    high, low = split(amplitude)
    both = dot(jnp.concatenate([high, low], axis=0), table(3))
    smoothed = both[: SEGS * ST] + both[SEGS * ST :]
    factor = column / (smoothed * (1.0 / (2 * WF + 1)) + 1e-06)
    return jnp.concatenate([real * factor, imag * factor], axis=1).astype(BF16)


def pack(raw, mask, order, mine, wanted, carried, order_here, mask_here, sems):
    half = raw.shape[1]
    away = (wanted, carried)
    copies = [
        pltpu.make_async_copy(order, order_here, sems.at[0]),
        pltpu.make_async_copy(mask, mask_here, sems.at[1]),
        pltpu.make_async_copy(raw, mine.at[:, pl.ds(0, half)], sems.at[2]),
    ]
    for copy in copies:
        copy.start()
    mine[:, half:] = jnp.zeros((ST, PAD), BF16)
    me = lax.axis_index("blk")
    copies[0].wait()
    for i, source in enumerate((lax.axis_index("section"), me & 1)):
        away[i][...] = jnp.full(away[i].shape, order_here[source] ^ me, jnp.int32)
    copies[1].wait()
    segs, stations = mask.shape
    mine[:segs, half : half + stations] = mask_here[...].astype(F32).astype(BF16)
    copies[2].wait()


def ordered(swap, one, two):
    one, two = one[...], two[...]
    return jnp.where(swap == 0, one, two), jnp.where(swap == 0, two, one)


def receivers(mine, other, *refs):
    tables, (white, masks, *held, sems) = refs[:6], refs[6:]
    copies = [pltpu.make_async_copy(t, h, sems.at[i]) for i, (t, h) in enumerate(zip(tables, held))]
    for copy in copies:
        copy.start()
    parts = ordered(lax.axis_index("section"), mine, other)
    column = mask_column(mask_rows(parts))
    masks[...] = jnp.broadcast_to(column, masks.shape)

    def table(i):
        copies[i].wait()
        return held[i][...]

    white[...] = whitened(parts, column, table)
    copies[4].wait()
    copies[5].wait()


def correlate(held, twin, white, masks, *refs):
    tables, out = refs[:-1], refs[-1]
    parts = ordered(lax.axis_index("blk") & 1, held, twin)
    sent_mask = mask_rows(parts)
    column = mask_column(sent_mask)
    sent = whitened(parts, column, lambda i: tables[i][...]).astype(F32)
    lag_high, lag_low = tables[4:]
    recv = white[...].astype(F32)
    size = SEGS * ST
    common = sum(masks[g * ST : (g + 1) * ST] * sent_mask[g : g + 1] for g in range(SEGS))
    rows, counts = [], []
    for n in range(ST):
        real = jnp.zeros((ST, NF), F32)
        imag = jnp.zeros((ST, NF), F32)
        for g in range(SEGS):
            line = sent[g * ST + n : g * ST + n + 1]
            tile = recv[g * ST : (g + 1) * ST]
            sr, si = line[:, :NF], line[:, NF:]
            rr, ri = tile[:, :NF], tile[:, NF:]
            real += rr * sr + ri * si
            imag += ri * sr - rr * si
        rows.append(jnp.concatenate([real, imag], axis=1))
        counts.append(common[:, n : n + 1])
    high, low = split(jnp.concatenate(rows, axis=0))
    both = dot(jnp.concatenate([high, low], axis=0), lag_high[...])
    lagged = both[:size] + both[size:] + dot(high, lag_low[...])
    lagged = lagged / jnp.maximum(jnp.concatenate(counts, axis=0), 1.0)
    out[...] = lagged.reshape(ST, ST, LAGS)


VMEM = pl.BlockSpec(memory_space=pltpu.VMEM)
HBM = pl.BlockSpec(memory_space=pltpu.HBM)


def call(body, out_shape, in_specs, arrays, scratch=(), flops=0):
    size = sum(a.size * a.dtype.itemsize for a in arrays)
    arrays = [
        pltpu.with_memory_space_constraint(a, pltpu.HBM) if spec is HBM else a
        for a, spec in zip(arrays, in_specs)
    ]
    return pl.pallas_call(
        body,
        out_shape=out_shape,
        in_specs=in_specs,
        out_specs=jax.tree.map(lambda _: VMEM, out_shape),
        scratch_shapes=scratch,
        cost_estimate=pl.CostEstimate(flops=flops, bytes_accessed=size, transcendentals=0),
        compiler_params=pltpu.CompilerParams(vmem_limit_bytes=16 * 1024 * 1024),
    )(*arrays)


def shaped(*shape, dtype=BF16):
    return jax.ShapeDtypeStruct(shape, dtype)


def exchange(x, flip, axis="blk"):
    devices = lax.axis_size(axis)
    return lax.ppermute(x, axis, [(i, i ^ flip) for i in range(devices)])


def crossing(x, bit):
    axes = ("section", "blk")
    blocks = lax.axis_size("blk")
    near, far = [], []
    for s in range(2):
        for b in range(blocks):
            here = s * blocks + b
            if s == b % 2:
                near.append((here, s * blocks + (b ^ bit)))
            else:
                there = (1 - s) * blocks
                near.append((here, there + (b ^ 1)))
                far.append((here, there + (b ^ 1 ^ bit)))
    return lax.ppermute(x, axes, near), lax.ppermute(x, axes, far)


def shards(raw_traces, valid_mask, block_order):
    section = lax.axis_index("section")
    blocks = lax.axis_size("blk")
    me = lax.axis_index("blk")
    core = me & 1
    half = raw_traces.shape[1]
    width = half + PAD
    mine, away_wanted, away_carried = call(
        pack,
        [shaped(ST, width)] + [shaped(ST, width, dtype=jnp.int32)] * 2,
        [HBM] * 3,
        [raw_traces, valid_mask.T, block_order],
        [
            pltpu.SMEM(block_order.shape, jnp.int32),
            pltpu.VMEM(valid_mask.shape[::-1], jnp.int32),
            pltpu.SemaphoreType.DMA((3,)),
        ],
    )

    raw_twin, mask_twin = exchange(raw_traces, 1), exchange(valid_mask.T, 1)
    raw_twin, mask_twin, mine, away_wanted, away_carried = lax.optimization_barrier((raw_twin, mask_twin, mine, away_wanted, away_carried))
    twin = lax.pad(raw_twin, jnp.zeros((), BF16), ((0, 0, 0), (0, PAD, 0)))
    rest = ((0, ST - valid_mask.shape[1], 0), (half, PAD - ST, 0))
    twin += lax.pad(mask_twin.astype(BF16), jnp.zeros((), BF16), rest)
    held = jnp.where(away_carried & 1 == 0, mine, twin)
    bits = [1 << i for i in range(1, blocks.bit_length() - 1)]
    last = bits.pop()
    other = None
    while bits:
        flips, bits = bits[:2], bits[2:]
        low, steps = flips[0], 1 << len(flips)
        got = [exchange(held, low * k) for k in range(1, steps)]
        if other is None:
            other = exchange(mine, 1, "section")
        rel = away_carried & (low * (steps - 1))
        for k in range(1, steps):
            held = jnp.where(rel == low * k, got[k - 1], held)
    tables = [filter_table(), mean_table(), forward_table(), smooth_table(), *lag_table()]
    tables = [jnp.asarray(t) for t in tables]
    near, far = crossing(held, last)
    white, masks, *tables = call(
        receivers,
        [shaped(SEGS * ST, 2 * NF), shaped(SEGS * ST, LANES, dtype=F32)]
        + [shaped(*t.shape) for t in tables],
        [VMEM] * 2 + [HBM] * len(tables),
        [mine, other, *tables],
        [pltpu.SemaphoreType.DMA((len(tables),))],
        flops=10**9,
    )
    near, far, white, masks = lax.optimization_barrier((near, far, white, masks))
    same = away_wanted & last == 0
    held = jnp.where(core == section, jnp.where(same, held, near), jnp.where(same, near, far))
    twin = exchange(held, 1)
    return call(
        correlate,
        shaped(ST, ST, LAGS, dtype=F32),
        [VMEM] * 10,
        [held, twin, white, masks, *tables],
        flops=10**9,
    )


def solution(mesh):
    return jax.shard_map(
        shards,
        mesh=mesh,
        in_specs=(P("blk", "section"), P("blk", "section"), P()),
        out_specs=P("section", "blk", None),
        check_vma=False,
    )
```

```python
import math

import jax
import jax.numpy as jnp
import numpy as np
from jax import lax
from jax.experimental import pallas as pl
from jax.experimental.pallas import tpu as pltpu
from jax.sharding import PartitionSpec as P

L = 1024
NF = 384
BIN_LO = 8
LAGS = 256
TAPS = 33
HW = 50
WF = 32
ST = 8
SEGS = 8
BLK = 256
ROWS = SEGS * L // BLK
PAD = 128
LANES = 128

EARLY = 3

F32 = jnp.float32
BF16 = jnp.bfloat16


def halves(table):
    high = table.astype(BF16)
    low = (table - high.astype(np.float64)).astype(BF16)
    return high, low


def band(values):
    reach = len(values) // 2
    shift = LANES + np.arange(LANES)[None, :] - np.arange(3 * LANES)[:, None] + reach
    inside = (shift >= 0) & (shift < len(values))
    return np.where(inside, values[np.clip(shift, 0, len(values) - 1)], 0.0)


def filter_table():
    k = np.arange(TAPS, dtype=np.float64) - (TAPS - 1) // 2
    low, high = BIN_LO / L, (BIN_LO + NF) / L
    window = 0.5 + 0.5 * np.cos(2.0 * math.pi * k / (TAPS + 1))
    taps = window * (2 * high * np.sinc(2 * high * k) - 2 * low * np.sinc(2 * low * k))
    return np.concatenate(halves(band(taps)), axis=1)


def mean_table():
    return band(np.ones(2 * HW + 1)).astype(BF16)


def smooth_table():
    return band(np.ones(2 * WF + 1)).astype(BF16)


def forward_table():
    phase = np.mod(np.arange(BLK)[:, None] * (BIN_LO + np.arange(NF))[None, :], L) * (2.0 * math.pi / L)
    return np.concatenate([np.cos(phase), -np.sin(phase)], axis=1).astype(BF16)


def lag_table():
    shifts = np.arange(LAGS // 2)[None, :]
    phase = np.mod((BIN_LO + np.arange(NF))[:, None] * shifts, L) * (2.0 * math.pi / L)
    table = np.concatenate([np.cos(phase), -np.sin(phase)], axis=0) / math.sqrt(NF)
    return halves(table)


def dot(a, b):
    return jnp.dot(a, b, preferred_element_type=F32)


def split(a):
    high = a.astype(BF16)
    return high, (a - high.astype(F32)).astype(BF16)


def spread(parts):
    rows = []
    for part in parts:
        half = part.shape[1] - PAD
        rows += [part[:, i * BLK : (i + 1) * BLK].astype(F32) for i in range(half // BLK)]
    return rows


def mask_rows(parts):
    per = (parts[0].shape[1] - PAD) // L
    return jnp.concatenate([p[:, p.shape[1] - PAD :].astype(F32)[:per] for p in parts], axis=0)


def mask_column(mask):
    diagonal = lax.broadcasted_iota(jnp.int32, (ST, LANES), 0) == lax.broadcasted_iota(
        jnp.int32, (ST, LANES), 1
    )
    tiles = [jnp.where(diagonal, mask[g : g + 1], 0.0) for g in range(SEGS)]
    return jnp.sum(jnp.concatenate(tiles, axis=0), axis=1, keepdims=True)


def quarters(parts):
    parts = parts.reshape(SEGS, L // BLK, ST, 2 * NF)
    q0, q1, q2, q3 = (parts[:, q].reshape(SEGS * ST, 2 * NF) for q in range(L // BLK))
    turn = (BIN_LO + lax.broadcasted_iota(jnp.int32, (1, 2 * NF), 1)) % 4
    even = turn % 2 == 0
    here = jnp.where(even, q0 + q2, q0 - q2)
    there = jnp.where(even, q1 + q3, q1 - q3)
    there = jnp.where(turn >= 2, -there, there)
    real, imag = there[:, :NF], there[:, NF:]
    even = even[:, :NF]
    return here[:, :NF] + jnp.where(even, real, imag), here[:, NF:] + jnp.where(even, imag, -real)


def whitened(parts, column, table):
    zero = jnp.zeros((2 * ST, BLK), F32)
    x = jnp.concatenate([zero, *spread(parts), zero], axis=0)
    n = x.shape[0]
    half = BLK // 2
    window = jnp.concatenate(
        [x[: n - 2 * ST, half:], x[ST : n - ST], x[2 * ST :, :half]], axis=1
    ).astype(BF16)
    taps = table(0)
    columns = []
    for i in range(2):
        both = dot(window[:, i * half : i * half + 3 * half], taps)
        columns.append(both[:, :half] + both[:, half:])
    filtered = jnp.concatenate(columns, axis=1)
    m = filtered.shape[0]
    size = jnp.abs(filtered)
    window = jnp.concatenate(
        [size[: m - 2 * ST, half:], size[ST : m - ST], size[2 * ST :, :half]], axis=1
    )
    high, low = split(window)
    mean, zero = table(1), jnp.zeros((half, half), BF16)
    mean = jnp.concatenate(
        [jnp.concatenate([mean, zero], axis=0), jnp.concatenate([zero, mean], axis=0)], axis=1
    )
    total = dot(high, mean) + dot(low, mean)
    normal = filtered[ST : m - ST] / (total * (1.0 / (2 * HW + 1)) + 1e-06)
    real, imag = quarters(dot(normal.astype(BF16), table(3)))
    amplitude = jnp.sqrt(real * real + imag * imag)
    high, low = split(amplitude)
    smooth = table(2)
    zero = jnp.zeros((half, half), BF16)
    smooth = jnp.concatenate(
        [
            jnp.concatenate([smooth[half:], zero], axis=0),
            smooth,
            jnp.concatenate([zero, smooth[: 2 * half]], axis=0),
        ],
        axis=1,
    )
    both = dot(jnp.concatenate([high, low], axis=0), smooth)
    smoothed = both[: SEGS * ST] + both[SEGS * ST :]
    factor = column / (smoothed * (1.0 / (2 * WF + 1)) + 1e-06)
    return jnp.concatenate([real * factor, imag * factor], axis=1).astype(BF16)


def pack(raw, mask, order, *refs):
    count = (len(refs) - 6) // 2
    tables, (mine, wanted, carried), held = refs[:count], refs[count : count + 3], refs[count + 3 : -3]
    order_here, mask_here, sems = refs[-3:]
    half = raw.shape[1]
    ends = [(order, order_here), (mask, mask_here), (raw, mine.at[:, pl.ds(0, half)]), *zip(tables, held)]
    copies = [pltpu.make_async_copy(a, b, sems.at[i]) for i, (a, b) in enumerate(ends)]
    for copy in copies:
        copy.start()
    mine[:, half:] = jnp.zeros((ST, PAD), BF16)
    me = lax.axis_index("blk")
    copies[0].wait()
    for away, source in ((wanted, lax.axis_index("section")), (carried, me & 1)):
        away[...] = jnp.full(away.shape, order_here[source] ^ me, jnp.int32)
    copies[1].wait()
    segs, stations = mask.shape
    mine[:segs, half : half + stations] = mask_here[...].astype(F32).astype(BF16)
    for copy in copies[2:]:
        copy.wait()


def ordered(swap, one, two):
    one, two = one[...], two[...]
    return jnp.where(swap == 0, one, two), jnp.where(swap == 0, two, one)


def receivers(mine, other, *refs):
    early, late, held, (white, masks, sems) = refs[:EARLY], refs[EARLY:6], refs[8:-1], (*refs[6:8], refs[-1])
    copies = [pltpu.make_async_copy(a, b, sems.at[i]) for i, (a, b) in enumerate(zip(late, held))]
    for copy in copies:
        copy.start()
    waiting = list(copies)

    def table(i):
        if i < EARLY:
            return early[i][...]
        copies[i - EARLY].wait()
        waiting.remove(copies[i - EARLY])
        return held[i - EARLY][...]

    parts = ordered(lax.axis_index("section"), mine, other)
    column = mask_column(mask_rows(parts))
    masks[...] = jnp.broadcast_to(column, masks.shape)
    white[...] = whitened(parts, column, table)
    for copy in waiting:
        copy.wait()


def correlate(held, twin, white, masks, *refs):
    tables, out = refs[:-1], refs[-1]
    parts = ordered(lax.axis_index("blk") & 1, held, twin)
    sent_mask = mask_rows(parts)
    column = mask_column(sent_mask)
    sent = whitened(parts, column, lambda i: tables[i][...]).astype(F32)
    lag_high, lag_low = tables[4:]
    recv = white[...].astype(F32)
    size = SEGS * ST
    common = sum(masks[g * ST : (g + 1) * ST] * sent_mask[g : g + 1] for g in range(SEGS))
    rows, counts = [], []
    for n in range(ST):
        real = jnp.zeros((ST, NF), F32)
        imag = jnp.zeros((ST, NF), F32)
        for g in range(SEGS):
            line = sent[g * ST + n : g * ST + n + 1]
            tile = recv[g * ST : (g + 1) * ST]
            sr, si = line[:, :NF], line[:, NF:]
            rr, ri = tile[:, :NF], tile[:, NF:]
            real += rr * sr + ri * si
            imag += ri * sr - rr * si
        rows.append(jnp.concatenate([real, imag], axis=1))
        counts.append(common[:, n : n + 1])
    stack = jnp.concatenate(rows, axis=0)
    bins = lax.broadcasted_iota(jnp.int32, (1, NF), 1) % 8
    cos = sum(jnp.where(bins == i, math.cos(math.pi * i / 4), 0.0) for i in range(8))
    sin = sum(jnp.where(bins == i, math.sin(math.pi * i / 4), 0.0) for i in range(8))
    real, imag = stack[:, :NF], stack[:, NF:]
    turned = jnp.concatenate([real * cos + imag * sin, imag * cos - real * sin], axis=1)
    high, low = split(jnp.concatenate([turned, stack], axis=0))
    both = dot(jnp.concatenate([high, low], axis=0), lag_high[...])
    lagged = both[: 2 * size] + both[2 * size :] + dot(high, lag_low[...])
    lagged = jnp.concatenate([lagged[:size], lagged[size:]], axis=1)
    lagged = lagged / jnp.maximum(jnp.concatenate(counts, axis=0), 1.0)
    out[...] = lagged.reshape(ST, ST, LAGS)


VMEM = pl.BlockSpec(memory_space=pltpu.VMEM)
HBM = pl.BlockSpec(memory_space=pltpu.HBM)


def call(body, out_shape, in_specs, arrays, scratch=(), flops=0):
    size = sum(a.size * a.dtype.itemsize for a in arrays)
    arrays = [
        pltpu.with_memory_space_constraint(a, pltpu.HBM) if spec is HBM else a
        for a, spec in zip(arrays, in_specs)
    ]
    return pl.pallas_call(
        body,
        out_shape=out_shape,
        in_specs=in_specs,
        out_specs=jax.tree.map(lambda _: VMEM, out_shape),
        scratch_shapes=scratch,
        cost_estimate=pl.CostEstimate(flops=flops, bytes_accessed=size, transcendentals=0),
        compiler_params=pltpu.CompilerParams(vmem_limit_bytes=16 * 1024 * 1024),
    )(*arrays)


def shaped(*shape, dtype=BF16):
    return jax.ShapeDtypeStruct(shape, dtype)


def exchange(x, flip, axis="blk"):
    devices = lax.axis_size(axis)
    return lax.ppermute(x, axis, [(i, i ^ flip) for i in range(devices)])


def crossing(x, bit):
    axes = ("section", "blk")
    blocks = lax.axis_size("blk")
    near, far = [], []
    for s in range(2):
        for b in range(blocks):
            here = s * blocks + b
            if s == b % 2:
                near.append((here, s * blocks + (b ^ bit)))
            else:
                there = (1 - s) * blocks
                near.append((here, there + (b ^ 1)))
                far.append((here, there + (b ^ 1 ^ bit)))
    return lax.ppermute(x, axes, near), lax.ppermute(x, axes, far)


def shards(raw_traces, valid_mask, block_order):
    section = lax.axis_index("section")
    blocks = lax.axis_size("blk")
    core = lax.axis_index("blk") & 1
    half = raw_traces.shape[1]
    width = half + PAD
    tables = [filter_table(), mean_table(), smooth_table(), forward_table(), *lag_table()]
    tables = [jnp.asarray(t) for t in tables]
    early, late = tables[:EARLY], tables[EARLY:]
    mine, away_wanted, away_carried, *early = call(
        pack,
        [shaped(ST, width)]
        + [shaped(ST, width, dtype=jnp.int32)] * 2
        + [shaped(*t.shape) for t in early],
        [HBM] * (3 + EARLY),
        [raw_traces, valid_mask.T, block_order, *early],
        [
            pltpu.SMEM(block_order.shape, jnp.int32),
            pltpu.VMEM(valid_mask.shape[::-1], jnp.int32),
            pltpu.SemaphoreType.DMA((3 + EARLY,)),
        ],
    )

    raw_twin, mask_twin, mine, away_wanted, away_carried = lax.optimization_barrier(
        (exchange(raw_traces, 1), exchange(valid_mask.T, 1), mine, away_wanted, away_carried)
    )
    nothing = jnp.zeros((), BF16)
    rest = ((0, ST - valid_mask.shape[1], 0), (half, PAD - ST, 0))
    twin = lax.pad(raw_twin, nothing, ((0, 0, 0), (0, PAD, 0)))
    twin += lax.pad(mask_twin.astype(BF16), nothing, rest)
    held = jnp.where(away_carried & 1 == 0, mine, twin)

    bits = [1 << i for i in range(1, blocks.bit_length() - 1)]
    last = bits.pop()
    near, far = crossing(held, last)
    other = exchange(mine, 1, "section")
    same = away_wanted & last == 0
    held = jnp.where(core == section, jnp.where(same, held, near), jnp.where(same, near, far))

    white = masks = None
    while bits:
        flips, bits = bits[:2], bits[2:]
        shifts = [flips[0] * k for k in range(1, 1 << len(flips))][::-1]
        got = [exchange(held, k) for k in shifts]
        if white is None:
            white, masks, *late = call(
                receivers,
                [shaped(SEGS * ST, 2 * NF), shaped(SEGS * ST, LANES, dtype=F32)]
                + [shaped(*t.shape) for t in late],
                [VMEM] * (2 + EARLY) + [HBM] * len(late),
                [mine, other, *early, *late],
                [pltpu.SemaphoreType.DMA((len(late),))],
                flops=10**9,
            )
            *got, white, masks = lax.optimization_barrier((*got, white, masks))
        rel = away_wanted & sum(flips)
        for k, piece in zip(shifts, got):
            held = jnp.where(rel == k, piece, held)
    twin = exchange(held, 1)
    return call(
        correlate,
        shaped(ST, ST, LAGS, dtype=F32),
        [VMEM] * 10,
        [held, twin, white, masks, *early, *late],
        flops=10**9,
    )


def solution(mesh):
    return jax.shard_map(
        shards,
        mesh=mesh,
        in_specs=(P("blk", "section"), P("blk", "section"), P()),
        out_specs=P("section", "blk", None),
        check_vma=False,
    )
```

```python
import math

import jax
import jax.numpy as jnp
import numpy as np
from jax import lax
from jax.experimental import pallas as pl
from jax.experimental.pallas import tpu as pltpu
from jax.sharding import PartitionSpec as P

L = 1024
NF = 384
BIN_LO = 8
LAGS = 256
TAPS = 33
HW = 50
WF = 32
ST = 8
SEGS = 8
BLK = 256
ROWS = SEGS * L // BLK
PAD = 128
LANES = 128

EARLY = 3

F32 = jnp.float32
BF16 = jnp.bfloat16


def halves(table):
    high = table.astype(BF16)
    low = (table - high.astype(np.float64)).astype(BF16)
    return high, low


def band(values):
    reach = len(values) // 2
    shift = LANES + np.arange(LANES)[None, :] - np.arange(3 * LANES)[:, None] + reach
    inside = (shift >= 0) & (shift < len(values))
    return np.where(inside, values[np.clip(shift, 0, len(values) - 1)], 0.0)


def filter_table():
    k = np.arange(TAPS, dtype=np.float64) - (TAPS - 1) // 2
    low, high = BIN_LO / L, (BIN_LO + NF) / L
    window = 0.5 + 0.5 * np.cos(2.0 * math.pi * k / (TAPS + 1))
    taps = window * (2 * high * np.sinc(2 * high * k) - 2 * low * np.sinc(2 * low * k))
    return np.concatenate(halves(band(taps)), axis=1)


def mean_table():
    return band(np.ones(2 * HW + 1)).astype(BF16)


def smooth_table():
    return band(np.ones(2 * WF + 1)).astype(BF16)


def forward_table():
    phase = np.mod(np.arange(BLK)[:, None] * (BIN_LO + np.arange(NF))[None, :], L) * (2.0 * math.pi / L)
    return np.concatenate([np.cos(phase), -np.sin(phase)], axis=1).astype(BF16)


def lag_table():
    shifts = np.arange(LAGS // 2)[None, :]
    phase = np.mod((BIN_LO + np.arange(NF))[:, None] * shifts, L) * (2.0 * math.pi / L)
    table = np.concatenate([np.cos(phase), -np.sin(phase)], axis=0) / math.sqrt(NF)
    return halves(table)


def dot(a, b):
    return jnp.dot(a, b, preferred_element_type=F32)


def split(a):
    high = a.astype(BF16)
    return high, (a - high.astype(F32)).astype(BF16)


def spread(parts):
    rows = []
    for part in parts:
        half = part.shape[1] - PAD
        rows += [part[:, i * BLK : (i + 1) * BLK].astype(F32) for i in range(half // BLK)]
    return rows


def mask_rows(parts):
    per = (parts[0].shape[1] - PAD) // L
    return jnp.concatenate([p[:, p.shape[1] - PAD :].astype(F32)[:per] for p in parts], axis=0)


def mask_column(mask):
    diagonal = lax.broadcasted_iota(jnp.int32, (ST, LANES), 0) == lax.broadcasted_iota(
        jnp.int32, (ST, LANES), 1
    )
    tiles = [jnp.where(diagonal, mask[g : g + 1], 0.0) for g in range(SEGS)]
    return jnp.sum(jnp.concatenate(tiles, axis=0), axis=1, keepdims=True)


def quarters(parts):
    parts = parts.reshape(SEGS, L // BLK, ST, 2 * NF)
    q0, q1, q2, q3 = (parts[:, q].reshape(SEGS * ST, 2 * NF) for q in range(L // BLK))
    turn = (BIN_LO + lax.broadcasted_iota(jnp.int32, (1, 2 * NF), 1)) % 4
    even = turn % 2 == 0
    here = jnp.where(even, q0 + q2, q0 - q2)
    there = jnp.where(even, q1 + q3, q1 - q3)
    there = jnp.where(turn >= 2, -there, there)
    real, imag = there[:, :NF], there[:, NF:]
    even = even[:, :NF]
    return here[:, :NF] + jnp.where(even, real, imag), here[:, NF:] + jnp.where(even, imag, -real)


def whitened(parts, column, table):
    zero = jnp.zeros((2 * ST, BLK), F32)
    x = jnp.concatenate([zero, *spread(parts), zero], axis=0)
    n = x.shape[0]
    half = BLK // 2
    window = jnp.concatenate(
        [x[: n - 2 * ST, half:], x[ST : n - ST], x[2 * ST :, :half]], axis=1
    ).astype(BF16)
    taps = table(0)
    columns = []
    for i in range(2):
        both = dot(window[:, i * half : i * half + 3 * half], taps)
        columns.append(both[:, :half] + both[:, half:])
    filtered = jnp.concatenate(columns, axis=1)
    m = filtered.shape[0]
    size = jnp.abs(filtered)
    window = jnp.concatenate(
        [size[: m - 2 * ST, half:], size[ST : m - ST], size[2 * ST :, :half]], axis=1
    )
    high, low = split(window)
    mean, zero = table(1), jnp.zeros((half, half), BF16)
    mean = jnp.concatenate(
        [jnp.concatenate([mean, zero], axis=0), jnp.concatenate([zero, mean], axis=0)], axis=1
    )
    total = dot(high, mean) + dot(low, mean)
    normal = filtered[ST : m - ST] / (total * (1.0 / (2 * HW + 1)) + 1e-06)
    real, imag = quarters(dot(normal.astype(BF16), table(3)))
    amplitude = jnp.sqrt(real * real + imag * imag)
    high, low = split(amplitude)
    smooth = table(2)
    zero = jnp.zeros((half, half), BF16)
    smooth = jnp.concatenate(
        [
            jnp.concatenate([smooth[half:], zero], axis=0),
            smooth,
            jnp.concatenate([zero, smooth[: 2 * half]], axis=0),
        ],
        axis=1,
    )
    both = dot(jnp.concatenate([high, low], axis=0), smooth)
    smoothed = both[: SEGS * ST] + both[SEGS * ST :]
    factor = column / (smoothed * (1.0 / (2 * WF + 1)) + 1e-06)
    return jnp.concatenate([real * factor, imag * factor], axis=1).astype(BF16)


def pack(raw, mask, order, *refs):
    count = (len(refs) - 6) // 2
    tables, (mine, wanted, carried), held = refs[:count], refs[count : count + 3], refs[count + 3 : -3]
    order_here, mask_here, sems = refs[-3:]
    half = raw.shape[1]
    ends = [(order, order_here), (mask, mask_here), (raw, mine.at[:, pl.ds(0, half)]), *zip(tables, held)]
    copies = [pltpu.make_async_copy(a, b, sems.at[i]) for i, (a, b) in enumerate(ends)]
    for copy in copies:
        copy.start()
    mine[:, half:] = jnp.zeros((ST, PAD), BF16)
    me = lax.axis_index("blk")
    copies[0].wait()
    for away, source in ((wanted, lax.axis_index("section")), (carried, me & 1)):
        away[...] = jnp.full(away.shape, order_here[source] ^ me, jnp.int32)
    copies[1].wait()
    segs, stations = mask.shape
    mine[:segs, half : half + stations] = mask_here[...].astype(F32).astype(BF16)
    for copy in copies[2:]:
        copy.wait()


def ordered(swap, one, two):
    one, two = one[...], two[...]
    return jnp.where(swap == 0, one, two), jnp.where(swap == 0, two, one)


def receivers(mine, other, *refs):
    early, late, held, (white, masks, sems) = refs[:EARLY], refs[EARLY:6], refs[8:-1], (*refs[6:8], refs[-1])
    copies = [pltpu.make_async_copy(a, b, sems.at[i]) for i, (a, b) in enumerate(zip(late, held))]
    for copy in copies:
        copy.start()
    waiting = list(copies)

    def table(i):
        if i < EARLY:
            return early[i][...]
        copies[i - EARLY].wait()
        waiting.remove(copies[i - EARLY])
        return held[i - EARLY][...]

    parts = ordered(lax.axis_index("section"), mine, other)
    column = mask_column(mask_rows(parts))
    masks[...] = jnp.broadcast_to(column, masks.shape)
    white[...] = whitened(parts, column, table)
    for copy in waiting:
        copy.wait()


def correlate(held, twin, white, masks, *refs):
    tables, out = refs[:-1], refs[-1]
    parts = ordered(lax.axis_index("blk") & 1, held, twin)
    sent_mask = mask_rows(parts)
    column = mask_column(sent_mask)
    sent = whitened(parts, column, lambda i: tables[i][...]).astype(F32)
    lag_high, lag_low = tables[4:]
    recv = white[...].astype(F32)
    size = SEGS * ST
    common = sum(masks[g * ST : (g + 1) * ST] * sent_mask[g : g + 1] for g in range(SEGS))
    rows, counts = [], []
    for n in range(ST):
        real = jnp.zeros((ST, NF), F32)
        imag = jnp.zeros((ST, NF), F32)
        for g in range(SEGS):
            line = sent[g * ST + n : g * ST + n + 1]
            tile = recv[g * ST : (g + 1) * ST]
            sr, si = line[:, :NF], line[:, NF:]
            rr, ri = tile[:, :NF], tile[:, NF:]
            real += rr * sr + ri * si
            imag += ri * sr - rr * si
        rows.append(jnp.concatenate([real, imag], axis=1))
        counts.append(common[:, n : n + 1])
    stack = jnp.concatenate(rows, axis=0)
    bins = lax.broadcasted_iota(jnp.int32, (1, NF), 1) % 8
    cos = sum(jnp.where(bins == i, math.cos(math.pi * i / 4), 0.0) for i in range(8))
    sin = sum(jnp.where(bins == i, math.sin(math.pi * i / 4), 0.0) for i in range(8))
    real, imag = stack[:, :NF], stack[:, NF:]
    turned = jnp.concatenate([real * cos + imag * sin, imag * cos - real * sin], axis=1)
    high, low = split(jnp.concatenate([turned, stack], axis=0))
    both = dot(jnp.concatenate([high, low], axis=0), lag_high[...])
    lagged = both[: 2 * size] + both[2 * size :] + dot(high, lag_low[...])
    lagged = jnp.concatenate([lagged[:size], lagged[size:]], axis=1)
    lagged = lagged / jnp.maximum(jnp.concatenate(counts, axis=0), 1.0)
    out[...] = lagged.reshape(ST, ST, LAGS)


VMEM = pl.BlockSpec(memory_space=pltpu.VMEM)
HBM = pl.BlockSpec(memory_space=pltpu.HBM)


def call(body, out_shape, in_specs, arrays, scratch=(), flops=0):
    size = sum(a.size * a.dtype.itemsize for a in arrays)
    arrays = [
        pltpu.with_memory_space_constraint(a, pltpu.HBM) if spec is HBM else a
        for a, spec in zip(arrays, in_specs)
    ]
    return pl.pallas_call(
        body,
        out_shape=out_shape,
        in_specs=in_specs,
        out_specs=jax.tree.map(lambda _: VMEM, out_shape),
        scratch_shapes=scratch,
        cost_estimate=pl.CostEstimate(flops=flops, bytes_accessed=size, transcendentals=0),
        compiler_params=pltpu.CompilerParams(vmem_limit_bytes=16 * 1024 * 1024),
    )(*arrays)


def shaped(*shape, dtype=BF16):
    return jax.ShapeDtypeStruct(shape, dtype)


def exchange(x, flip, axis="blk"):
    devices = lax.axis_size(axis)
    return lax.ppermute(x, axis, [(i, i ^ flip) for i in range(devices)])


def crossing(x, bit):
    axes = ("section", "blk")
    blocks = lax.axis_size("blk")
    near, far = [], []
    for s in range(2):
        for b in range(blocks):
            here, there = s * blocks, (1 - s) * blocks
            if s == b % 2:
                near.append((here + b, here + (b ^ bit)))
                far.append((here + b, there + (b ^ 1)))
            else:
                near.append((here + b, there + (b ^ 1)))
                far.append((here + b, there + (b ^ 1 ^ bit)))
    return lax.ppermute(x, axes, near), lax.ppermute(x, axes, far)


def shards(raw_traces, valid_mask, block_order):
    section = lax.axis_index("section")
    blocks = lax.axis_size("blk")
    core = lax.axis_index("blk") & 1
    half = raw_traces.shape[1]
    width = half + PAD
    tables = [filter_table(), mean_table(), smooth_table(), forward_table(), *lag_table()]
    tables = [jnp.asarray(t) for t in tables]
    early, late = tables[:EARLY], tables[EARLY:]
    mine, away_wanted, away_carried, *early = call(
        pack,
        [shaped(ST, width)]
        + [shaped(ST, width, dtype=jnp.int32)] * 2
        + [shaped(*t.shape) for t in early],
        [HBM] * (3 + EARLY),
        [raw_traces, valid_mask.T, block_order, *early],
        [
            pltpu.SMEM(block_order.shape, jnp.int32),
            pltpu.VMEM(valid_mask.shape[::-1], jnp.int32),
            pltpu.SemaphoreType.DMA((3 + EARLY,)),
        ],
    )

    raw_twin, mask_twin, mine, away_wanted, away_carried = lax.optimization_barrier(
        (exchange(raw_traces, 1), exchange(valid_mask.T, 1), mine, away_wanted, away_carried)
    )
    nothing = jnp.zeros((), BF16)
    rest = ((0, ST - valid_mask.shape[1], 0), (half, PAD - ST, 0))
    twin = lax.pad(raw_twin, nothing, ((0, 0, 0), (0, PAD, 0)))
    twin += lax.pad(mask_twin.astype(BF16), nothing, rest)
    held = jnp.where(away_carried & 1 == 0, mine, twin)

    bits = [1 << i for i in range(1, blocks.bit_length() - 1)]
    last = bits.pop()
    near, far = crossing(held, last)
    other = exchange(mine, 1, "section")
    same = away_wanted & last == 0
    held = jnp.where(core == section, jnp.where(same, held, near), jnp.where(same, near, far))

    white = masks = None
    while bits:
        flips, bits = bits[:2], bits[2:]
        shifts = [flips[0] * k for k in range(1, 1 << len(flips))][::-1]
        got = [exchange(held, k) for k in shifts]
        if white is None:
            white, masks, *late = call(
                receivers,
                [shaped(SEGS * ST, 2 * NF), shaped(SEGS * ST, LANES, dtype=F32)]
                + [shaped(*t.shape) for t in late],
                [VMEM] * (2 + EARLY) + [HBM] * len(late),
                [mine, other, *early, *late],
                [pltpu.SemaphoreType.DMA((len(late),))],
                flops=10**9,
            )
            *got, white, masks = lax.optimization_barrier((*got, white, masks))
        rel = away_wanted & sum(flips)
        for k, piece in zip(shifts, got):
            held = jnp.where(rel == k, piece, held)
    twin = exchange(held, 1)
    return call(
        correlate,
        shaped(ST, ST, LAGS, dtype=F32),
        [VMEM] * 10,
        [held, twin, white, masks, *early, *late],
        flops=10**9,
    )


def solution(mesh):
    return jax.shard_map(
        shards,
        mesh=mesh,
        in_specs=(P("blk", "section"), P("blk", "section"), P()),
        out_specs=P("section", "blk", None),
        check_vma=False,
    )
```

```python
import math

import jax
import jax.numpy as jnp
import numpy as np
from jax import lax
from jax.experimental import pallas as pl
from jax.experimental.pallas import tpu as pltpu
from jax.sharding import PartitionSpec as P

L = 1024
NF = 384
BIN_LO = 8
LAGS = 256
TAPS = 33
HW = 50
WF = 32
ST = 8
SEGS = 8
BLK = 256
ROWS = SEGS * L // BLK
PAD = 128
LANES = 128

F32 = jnp.float32
BF16 = jnp.bfloat16


def halves(table):
    high = table.astype(BF16)
    low = (table - high.astype(np.float64)).astype(BF16)
    return high, low


def band(values):
    reach = len(values) // 2
    shift = LANES + np.arange(LANES)[None, :] - np.arange(3 * LANES)[:, None] + reach
    inside = (shift >= 0) & (shift < len(values))
    return np.where(inside, values[np.clip(shift, 0, len(values) - 1)], 0.0)


def filter_table():
    k = np.arange(TAPS, dtype=np.float64) - (TAPS - 1) // 2
    low, high = BIN_LO / L, (BIN_LO + NF) / L
    window = 0.5 + 0.5 * np.cos(2.0 * math.pi * k / (TAPS + 1))
    taps = window * (2 * high * np.sinc(2 * high * k) - 2 * low * np.sinc(2 * low * k))
    return np.concatenate(halves(band(taps)), axis=1)


def mean_table():
    return band(np.ones(2 * HW + 1)).astype(BF16)


def smooth_table():
    return band(np.ones(2 * WF + 1)).astype(BF16)


def forward_table():
    phase = np.mod(np.arange(BLK)[:, None] * (BIN_LO + np.arange(NF))[None, :], L) * (2.0 * math.pi / L)
    return np.concatenate([np.cos(phase), -np.sin(phase)], axis=1).astype(BF16)


def lag_table():
    shifts = np.arange(LAGS // 2)[None, :]
    phase = np.mod((BIN_LO + np.arange(NF))[:, None] * shifts, L) * (2.0 * math.pi / L)
    table = np.concatenate([np.cos(phase), -np.sin(phase)], axis=0) / math.sqrt(NF)
    return halves(table)


def dot(a, b):
    return jnp.dot(a, b, preferred_element_type=F32)


def split(a):
    high = a.astype(BF16)
    return high, (a - high.astype(F32)).astype(BF16)


def spread(parts):
    rows = []
    for part in parts:
        half = part.shape[1] - PAD
        rows += [part[:, i * BLK : (i + 1) * BLK].astype(F32) for i in range(half // BLK)]
    return rows


def mask_rows(parts):
    per = (parts[0].shape[1] - PAD) // L
    return jnp.concatenate([p[:, p.shape[1] - PAD :].astype(F32)[:per] for p in parts], axis=0)


def mask_column(mask):
    diagonal = lax.broadcasted_iota(jnp.int32, (ST, LANES), 0) == lax.broadcasted_iota(
        jnp.int32, (ST, LANES), 1
    )
    tiles = [jnp.where(diagonal, mask[g : g + 1], 0.0) for g in range(SEGS)]
    return jnp.sum(jnp.concatenate(tiles, axis=0), axis=1, keepdims=True)


def quarters(parts):
    parts = parts.reshape(SEGS, L // BLK, ST, 2 * NF)
    q0, q1, q2, q3 = (parts[:, q].reshape(SEGS * ST, 2 * NF) for q in range(L // BLK))
    turn = (BIN_LO + lax.broadcasted_iota(jnp.int32, (1, 2 * NF), 1)) % 4
    even = turn % 2 == 0
    here = jnp.where(even, q0 + q2, q0 - q2)
    there = jnp.where(even, q1 + q3, q1 - q3)
    there = jnp.where(turn >= 2, -there, there)
    real, imag = there[:, :NF], there[:, NF:]
    even = even[:, :NF]
    return here[:, :NF] + jnp.where(even, real, imag), here[:, NF:] + jnp.where(even, imag, -real)


def whitened(parts, column, table):
    zero = jnp.zeros((2 * ST, BLK), F32)
    x = jnp.concatenate([zero, *spread(parts), zero], axis=0)
    n = x.shape[0]
    half = BLK // 2
    window = jnp.concatenate(
        [x[: n - 2 * ST, half:], x[ST : n - ST], x[2 * ST :, :half]], axis=1
    ).astype(BF16)
    taps = table(0)
    columns = []
    for i in range(2):
        both = dot(window[:, i * half : i * half + 3 * half], taps)
        columns.append(both[:, :half] + both[:, half:])
    filtered = jnp.concatenate(columns, axis=1)
    m = filtered.shape[0]
    size = jnp.abs(filtered)
    window = jnp.concatenate(
        [size[: m - 2 * ST, half:], size[ST : m - ST], size[2 * ST :, :half]], axis=1
    )
    high, low = split(window)
    mean, zero = table(1), jnp.zeros((half, half), BF16)
    mean = jnp.concatenate(
        [jnp.concatenate([mean, zero], axis=0), jnp.concatenate([zero, mean], axis=0)], axis=1
    )
    total = dot(high, mean) + dot(low, mean)
    normal = filtered[ST : m - ST] / (total * (1.0 / (2 * HW + 1)) + 1e-06)
    real, imag = quarters(dot(normal.astype(BF16), table(3)))
    amplitude = jnp.sqrt(real * real + imag * imag)
    high, low = split(amplitude)
    smooth = table(2)
    zero = jnp.zeros((half, half), BF16)
    smooth = jnp.concatenate(
        [
            jnp.concatenate([smooth[half:], zero], axis=0),
            smooth,
            jnp.concatenate([zero, smooth[: 2 * half]], axis=0),
        ],
        axis=1,
    )
    both = dot(jnp.concatenate([high, low], axis=0), smooth)
    smoothed = both[: SEGS * ST] + both[SEGS * ST :]
    factor = column / (smoothed * (1.0 / (2 * WF + 1)) + 1e-06)
    return jnp.concatenate([real * factor, imag * factor], axis=1).astype(BF16)


def pack(raw, mask, order, mine, wanted, carried, order_here, mask_here, sems):
    half = raw.shape[1]
    ends = [(order, order_here), (mask, mask_here), (raw, mine.at[:, pl.ds(0, half)])]
    copies = [pltpu.make_async_copy(a, b, sems.at[i]) for i, (a, b) in enumerate(ends)]
    for copy in copies:
        copy.start()
    mine[:, half:] = jnp.zeros((ST, PAD), BF16)
    me = lax.axis_index("blk")
    copies[0].wait()
    for away, source in ((wanted, lax.axis_index("section")), (carried, me & 1)):
        away[...] = jnp.full(away.shape, order_here[source] ^ me, jnp.int32)
    copies[1].wait()
    segs, stations = mask.shape
    mine[:segs, half : half + stations] = mask_here[...].astype(F32).astype(BF16)
    copies[2].wait()


def ordered(swap, one, two):
    one, two = one[...], two[...]
    return jnp.where(swap == 0, one, two), jnp.where(swap == 0, two, one)


def receivers(mine, other, *refs):
    tables, (white, masks), held, sems = refs[:6], refs[6:8], refs[8:14], refs[14]
    copies = [pltpu.make_async_copy(a, b, sems.at[i]) for i, (a, b) in enumerate(zip(tables, held))]
    for copy in copies:
        copy.start()

    def table(i):
        copies[i].wait()
        return held[i][...]

    parts = ordered(lax.axis_index("section"), mine, other)
    column = mask_column(mask_rows(parts))
    masks[...] = jnp.broadcast_to(column, masks.shape)
    white[...] = whitened(parts, column, table)
    for copy in copies[4:]:
        copy.wait()


def correlate(held, twin, white, masks, *refs):
    tables, out = refs[:-1], refs[-1]
    parts = ordered(lax.axis_index("blk") & 1, held, twin)
    sent_mask = mask_rows(parts)
    column = mask_column(sent_mask)
    sent = whitened(parts, column, lambda i: tables[i][...]).astype(F32)
    lag_high, lag_low = tables[4:]
    recv = white[...].astype(F32)
    size = SEGS * ST
    common = sum(masks[g * ST : (g + 1) * ST] * sent_mask[g : g + 1] for g in range(SEGS))
    rows, counts = [], []
    for n in range(ST):
        real = jnp.zeros((ST, NF), F32)
        imag = jnp.zeros((ST, NF), F32)
        for g in range(SEGS):
            line = sent[g * ST + n : g * ST + n + 1]
            tile = recv[g * ST : (g + 1) * ST]
            sr, si = line[:, :NF], line[:, NF:]
            rr, ri = tile[:, :NF], tile[:, NF:]
            real += rr * sr + ri * si
            imag += ri * sr - rr * si
        rows.append(jnp.concatenate([real, imag], axis=1))
        counts.append(common[:, n : n + 1])
    stack = jnp.concatenate(rows, axis=0)
    bins = lax.broadcasted_iota(jnp.int32, (1, NF), 1) % 8
    cos = sum(jnp.where(bins == i, math.cos(math.pi * i / 4), 0.0) for i in range(8))
    sin = sum(jnp.where(bins == i, math.sin(math.pi * i / 4), 0.0) for i in range(8))
    real, imag = stack[:, :NF], stack[:, NF:]
    turned = jnp.concatenate([real * cos + imag * sin, imag * cos - real * sin], axis=1)
    high, low = split(jnp.concatenate([turned, stack], axis=0))
    both = dot(jnp.concatenate([high, low], axis=0), lag_high[...])
    lagged = both[: 2 * size] + both[2 * size :] + dot(high, lag_low[...])
    lagged = jnp.concatenate([lagged[:size], lagged[size:]], axis=1)
    lagged = lagged / jnp.maximum(jnp.concatenate(counts, axis=0), 1.0)
    out[...] = lagged.reshape(ST, ST, LAGS)


VMEM = pl.BlockSpec(memory_space=pltpu.VMEM)
HBM = pl.BlockSpec(memory_space=pltpu.HBM)


def call(body, out_shape, in_specs, arrays, scratch=(), flops=0):
    size = sum(a.size * a.dtype.itemsize for a in arrays)
    arrays = [
        pltpu.with_memory_space_constraint(a, pltpu.HBM) if spec is HBM else a
        for a, spec in zip(arrays, in_specs)
    ]
    return pl.pallas_call(
        body,
        out_shape=out_shape,
        in_specs=in_specs,
        out_specs=jax.tree.map(lambda _: VMEM, out_shape),
        scratch_shapes=scratch,
        cost_estimate=pl.CostEstimate(flops=flops, bytes_accessed=size, transcendentals=0),
        compiler_params=pltpu.CompilerParams(vmem_limit_bytes=16 * 1024 * 1024),
    )(*arrays)


def shaped(*shape, dtype=BF16):
    return jax.ShapeDtypeStruct(shape, dtype)


def exchange(x, flip, axis="blk"):
    devices = lax.axis_size(axis)
    return lax.ppermute(x, axis, [(i, i ^ flip) for i in range(devices)])


def crossing(x, bit):
    axes = ("section", "blk")
    blocks = lax.axis_size("blk")
    near, far = [], []
    for s in range(2):
        for b in range(blocks):
            here, there = s * blocks, (1 - s) * blocks
            if s == b % 2:
                near.append((here + b, here + (b ^ bit)))
                far.append((here + b, there + (b ^ 1)))
            else:
                near.append((here + b, there + (b ^ 1)))
                far.append((here + b, there + (b ^ 1 ^ bit)))
    return lax.ppermute(x, axes, near), lax.ppermute(x, axes, far)


def shards(raw_traces, valid_mask, block_order):
    section = lax.axis_index("section")
    blocks = lax.axis_size("blk")
    core = lax.axis_index("blk") & 1
    half = raw_traces.shape[1]
    width = half + PAD
    tables = [filter_table(), mean_table(), smooth_table(), forward_table(), *lag_table()]
    tables = [jnp.asarray(t) for t in tables]
    mine, away_wanted, away_carried = call(
        pack,
        [shaped(ST, width)] + [shaped(ST, width, dtype=jnp.int32)] * 2,
        [HBM] * 3,
        [raw_traces, valid_mask.T, block_order],
        [
            pltpu.SMEM(block_order.shape, jnp.int32),
            pltpu.VMEM(valid_mask.shape[::-1], jnp.int32),
            pltpu.SemaphoreType.DMA((3,)),
        ],
    )

    raw_twin, mask_twin, mine, away_wanted, away_carried = lax.optimization_barrier(
        (exchange(raw_traces, 1), exchange(valid_mask.T, 1), mine, away_wanted, away_carried)
    )
    nothing = jnp.zeros((), BF16)
    rest = ((0, ST - valid_mask.shape[1], 0), (half, PAD - ST, 0))
    twin = lax.pad(raw_twin, nothing, ((0, 0, 0), (0, PAD, 0)))
    twin += lax.pad(mask_twin.astype(BF16), nothing, rest)
    held = jnp.where(away_carried & 1 == 0, mine, twin)

    bits = [1 << i for i in range(1, blocks.bit_length() - 1)]
    last = bits.pop()
    near, far = crossing(held, last)
    other = exchange(mine, 1, "section")
    same = away_wanted & last == 0
    far, near = lax.optimization_barrier((far, near))
    held = jnp.where(core == section, jnp.where(same, held, near), jnp.where(same, near, far))

    white = masks = None
    while bits:
        flips, bits = bits[:2], bits[2:]
        shifts = [flips[0] * k for k in range(1, 1 << len(flips))]
        got = [exchange(held, k) for k in shifts]
        if white is None:
            white, masks, *tables = call(
                receivers,
                [shaped(SEGS * ST, 2 * NF), shaped(SEGS * ST, LANES, dtype=F32)]
                + [shaped(*t.shape) for t in tables],
                [VMEM] * 2 + [HBM] * len(tables),
                [mine, other, *tables],
                [pltpu.SemaphoreType.DMA((len(tables),))],
                flops=10**9,
            )
            *got, white, masks = lax.optimization_barrier((*got, white, masks))
        rel = away_wanted & sum(flips)
        for k, piece in zip(shifts, got):
            held = jnp.where(rel == k, piece, held)
    twin = exchange(held, 1)
    return call(
        correlate,
        shaped(ST, ST, LAGS, dtype=F32),
        [VMEM] * 10,
        [held, twin, white, masks, *tables],
        flops=10**9,
    )


def solution(mesh):
    return jax.shard_map(
        shards,
        mesh=mesh,
        in_specs=(P("blk", "section"), P("blk", "section"), P()),
        out_specs=P("section", "blk", None),
        check_vma=False,
    )
```

```python
import math

import jax
import jax.numpy as jnp
import numpy as np
from jax import lax
from jax.experimental import pallas as pl
from jax.experimental.pallas import tpu as pltpu
from jax.sharding import PartitionSpec as P

L = 1024
NF = 384
BIN_LO = 8
LAGS = 256
TAPS = 33
HW = 50
WF = 32
ST = 8
SEGS = 8
BLK = 256
ROWS = SEGS * L // BLK
PAD = 128
LANES = 128

F32 = jnp.float32
BF16 = jnp.bfloat16


def halves(table):
    high = table.astype(BF16)
    low = (table - high.astype(np.float64)).astype(BF16)
    return high, low


def band(values):
    reach = len(values) // 2
    shift = LANES + np.arange(LANES)[None, :] - np.arange(3 * LANES)[:, None] + reach
    inside = (shift >= 0) & (shift < len(values))
    return np.where(inside, values[np.clip(shift, 0, len(values) - 1)], 0.0)


def filter_table():
    k = np.arange(TAPS, dtype=np.float64) - (TAPS - 1) // 2
    low, high = BIN_LO / L, (BIN_LO + NF) / L
    window = 0.5 + 0.5 * np.cos(2.0 * math.pi * k / (TAPS + 1))
    taps = window * (2 * high * np.sinc(2 * high * k) - 2 * low * np.sinc(2 * low * k))
    return np.concatenate(halves(band(taps)), axis=1)


def mean_table():
    return band(np.ones(2 * HW + 1)).astype(BF16)


def smooth_table():
    return band(np.ones(2 * WF + 1)).astype(BF16)


def forward_table():
    phase = np.mod(np.arange(BLK)[:, None] * (BIN_LO + np.arange(NF))[None, :], L) * (2.0 * math.pi / L)
    return np.concatenate([np.cos(phase), -np.sin(phase)], axis=1).astype(BF16)


def lag_table():
    shifts = np.arange(LAGS // 2)[None, :]
    phase = np.mod((BIN_LO + np.arange(NF))[:, None] * shifts, L) * (2.0 * math.pi / L)
    table = np.concatenate([np.cos(phase), -np.sin(phase)], axis=0) / math.sqrt(NF)
    return halves(table)


def dot(a, b):
    return jnp.dot(a, b, preferred_element_type=F32)


def split(a):
    high = a.astype(BF16)
    return high, (a - high.astype(F32)).astype(BF16)


def spread(parts):
    rows = []
    for part in parts:
        half = part.shape[1] - PAD
        rows += [part[:, i * BLK : (i + 1) * BLK].astype(F32) for i in range(half // BLK)]
    return rows


def mask_rows(parts):
    per = (parts[0].shape[1] - PAD) // L
    return jnp.concatenate([p[:, p.shape[1] - PAD :].astype(F32)[:per] for p in parts], axis=0)


def mask_column(mask):
    diagonal = lax.broadcasted_iota(jnp.int32, (ST, LANES), 0) == lax.broadcasted_iota(
        jnp.int32, (ST, LANES), 1
    )
    tiles = [jnp.where(diagonal, mask[g : g + 1], 0.0) for g in range(SEGS)]
    return jnp.sum(jnp.concatenate(tiles, axis=0), axis=1, keepdims=True)


def quarters(parts):
    parts = parts.reshape(SEGS, L // BLK, ST, 2 * NF)
    q0, q1, q2, q3 = (parts[:, q].reshape(SEGS * ST, 2 * NF) for q in range(L // BLK))
    turn = (BIN_LO + lax.broadcasted_iota(jnp.int32, (1, 2 * NF), 1)) % 4
    even = turn % 2 == 0
    here = jnp.where(even, q0 + q2, q0 - q2)
    there = jnp.where(even, q1 + q3, q1 - q3)
    there = jnp.where(turn >= 2, -there, there)
    real, imag = there[:, :NF], there[:, NF:]
    even = even[:, :NF]
    return here[:, :NF] + jnp.where(even, real, imag), here[:, NF:] + jnp.where(even, imag, -real)


def whitened(parts, column, table):
    zero = jnp.zeros((2 * ST, BLK), F32)
    x = jnp.concatenate([zero, *spread(parts), zero], axis=0)
    n = x.shape[0]
    half = BLK // 2
    window = jnp.concatenate(
        [x[: n - 2 * ST, half:], x[ST : n - ST], x[2 * ST :, :half]], axis=1
    ).astype(BF16)
    taps = table(0)
    columns = []
    for i in range(2):
        both = dot(window[:, i * half : i * half + 3 * half], taps)
        columns.append(both[:, :half] + both[:, half:])
    filtered = jnp.concatenate(columns, axis=1)
    m = filtered.shape[0]
    size = jnp.abs(filtered)
    window = jnp.concatenate(
        [size[: m - 2 * ST, half:], size[ST : m - ST], size[2 * ST :, :half]], axis=1
    )
    high, low = split(window)
    mean, zero = table(1), jnp.zeros((half, half), BF16)
    mean = jnp.concatenate(
        [jnp.concatenate([mean, zero], axis=0), jnp.concatenate([zero, mean], axis=0)], axis=1
    )
    both = dot(jnp.concatenate([high, low], axis=0), mean)
    total = both[: both.shape[0] // 2] + both[both.shape[0] // 2 :]
    normal = filtered[ST : m - ST] / (total * (1.0 / (2 * HW + 1)) + 1e-06)
    real, imag = quarters(dot(normal.astype(BF16), table(3)))
    amplitude = jnp.sqrt(real * real + imag * imag)
    high, low = split(amplitude)
    smooth = table(2)
    zero = jnp.zeros((half, half), BF16)
    smooth = jnp.concatenate(
        [
            jnp.concatenate([smooth[half:], zero], axis=0),
            smooth,
            jnp.concatenate([zero, smooth[: 2 * half]], axis=0),
        ],
        axis=1,
    )
    both = dot(jnp.concatenate([high, low], axis=0), smooth)
    smoothed = both[: SEGS * ST] + both[SEGS * ST :]
    factor = column / (smoothed * (1.0 / (2 * WF + 1)) + 1e-06)
    return jnp.concatenate([real * factor, imag * factor], axis=1).astype(BF16)


def pack(raw, mask, order, mine, wanted, carried, order_here, mask_here, sems):
    half = raw.shape[1]
    ends = [(order, order_here), (mask, mask_here), (raw, mine.at[:, pl.ds(0, half)])]
    copies = [pltpu.make_async_copy(a, b, sems.at[i]) for i, (a, b) in enumerate(ends)]
    for copy in copies:
        copy.start()
    mine[:, half:] = jnp.zeros((ST, PAD), BF16)
    me = lax.axis_index("blk")
    copies[0].wait()
    for away, source in ((wanted, lax.axis_index("section")), (carried, me & 1)):
        away[...] = jnp.full(away.shape, order_here[source] ^ me, jnp.int32)
    copies[1].wait()
    segs, stations = mask.shape
    mine[:segs, half : half + stations] = mask_here[...].astype(F32).astype(BF16)
    copies[2].wait()


def ordered(swap, one, two):
    one, two = one[...], two[...]
    return jnp.where(swap == 0, one, two), jnp.where(swap == 0, two, one)


def receivers(mine, other, *refs):
    tables, (white, masks), held, sems = refs[:6], refs[6:8], refs[8:14], refs[14]
    copies = [pltpu.make_async_copy(a, b, sems.at[i]) for i, (a, b) in enumerate(zip(tables, held))]
    for copy in copies:
        copy.start()

    def table(i):
        copies[i].wait()
        return held[i][...]

    parts = ordered(lax.axis_index("section"), mine, other)
    column = mask_column(mask_rows(parts))
    masks[...] = jnp.broadcast_to(column, masks.shape)
    white[...] = whitened(parts, column, table)
    for copy in copies[4:]:
        copy.wait()


def correlate(held, twin, white, masks, *refs):
    tables, out = refs[:-1], refs[-1]
    parts = ordered(lax.axis_index("blk") & 1, held, twin)
    sent_mask = mask_rows(parts)
    column = mask_column(sent_mask)
    sent = whitened(parts, column, lambda i: tables[i][...]).astype(F32)
    lag_high, lag_low = tables[4:]
    recv = white[...].astype(F32)
    size = SEGS * ST
    common = sum(masks[g * ST : (g + 1) * ST] * sent_mask[g : g + 1] for g in range(SEGS))
    rows, counts = [], []
    for n in range(ST):
        real = jnp.zeros((ST, NF), F32)
        imag = jnp.zeros((ST, NF), F32)
        for g in range(SEGS):
            line = sent[g * ST + n : g * ST + n + 1]
            tile = recv[g * ST : (g + 1) * ST]
            sr, si = line[:, :NF], line[:, NF:]
            rr, ri = tile[:, :NF], tile[:, NF:]
            real += rr * sr + ri * si
            imag += ri * sr - rr * si
        rows.append(jnp.concatenate([real, imag], axis=1))
        counts.append(common[:, n : n + 1])
    stack = jnp.concatenate(rows, axis=0)
    bins = lax.broadcasted_iota(jnp.int32, (1, NF), 1) % 8
    cos = sum(jnp.where(bins == i, math.cos(math.pi * i / 4), 0.0) for i in range(8))
    sin = sum(jnp.where(bins == i, math.sin(math.pi * i / 4), 0.0) for i in range(8))
    real, imag = stack[:, :NF], stack[:, NF:]
    turned = jnp.concatenate([real * cos + imag * sin, imag * cos - real * sin], axis=1)
    high, low = split(jnp.concatenate([turned, stack], axis=0))
    both = dot(jnp.concatenate([high, low], axis=0), lag_high[...])
    lagged = both[: 2 * size] + both[2 * size :] + dot(high, lag_low[...])
    lagged = jnp.concatenate([lagged[:size], lagged[size:]], axis=1)
    lagged = lagged / jnp.maximum(jnp.concatenate(counts, axis=0), 1.0)
    out[...] = lagged.reshape(ST, ST, LAGS)


VMEM = pl.BlockSpec(memory_space=pltpu.VMEM)
HBM = pl.BlockSpec(memory_space=pltpu.HBM)


def call(body, out_shape, in_specs, arrays, scratch=(), flops=0, fused=None):
    size = sum(a.size * a.dtype.itemsize for a in arrays)
    arrays = [
        pltpu.with_memory_space_constraint(a, pltpu.HBM) if spec is HBM else a
        for a, spec in zip(arrays, in_specs)
    ]
    return pl.pallas_call(
        body,
        out_shape=out_shape,
        in_specs=in_specs,
        out_specs=jax.tree.map(lambda _: VMEM, out_shape),
        scratch_shapes=scratch,
        cost_estimate=pl.CostEstimate(flops=flops, bytes_accessed=size, transcendentals=0),
        compiler_params=pltpu.CompilerParams(vmem_limit_bytes=16 * 1024 * 1024, allow_input_fusion=fused),
    )(*arrays)


def shaped(*shape, dtype=BF16):
    return jax.ShapeDtypeStruct(shape, dtype)


def exchange(x, flip, axis="blk"):
    devices = lax.axis_size(axis)
    return lax.ppermute(x, axis, [(i, i ^ flip) for i in range(devices)])


def crossing(x, bit):
    axes = ("section", "blk")
    blocks = lax.axis_size("blk")
    near, far = [], []
    for s in range(2):
        for b in range(blocks):
            here, there = s * blocks, (1 - s) * blocks
            if s == b % 2:
                near.append((here + b, here + (b ^ bit)))
                far.append((here + b, there + (b ^ 1)))
            else:
                near.append((here + b, there + (b ^ 1)))
                far.append((here + b, there + (b ^ 1 ^ bit)))
    return lax.ppermute(x, axes, near), lax.ppermute(x, axes, far)


def shards(raw_traces, valid_mask, block_order):
    section = lax.axis_index("section")
    blocks = lax.axis_size("blk")
    core = lax.axis_index("blk") & 1
    half = raw_traces.shape[1]
    width = half + PAD
    tables = [filter_table(), mean_table(), smooth_table(), forward_table(), *lag_table()]
    tables = [jnp.asarray(t) for t in tables]
    mine, away_wanted, away_carried = call(
        pack,
        [shaped(ST, width)] + [shaped(ST, width, dtype=jnp.int32)] * 2,
        [HBM] * 3,
        [raw_traces, valid_mask.T, block_order],
        [
            pltpu.SMEM(block_order.shape, jnp.int32),
            pltpu.VMEM(valid_mask.shape[::-1], jnp.int32),
            pltpu.SemaphoreType.DMA((3,)),
        ],
    )

    raw_twin, mask_twin, mine, away_wanted, away_carried = lax.optimization_barrier(
        (exchange(raw_traces, 1), exchange(valid_mask.T, 1), mine, away_wanted, away_carried)
    )
    nothing = jnp.zeros((), BF16)
    rest = ((0, ST - valid_mask.shape[1], 0), (half, PAD - ST, 0))
    twin = lax.pad(raw_twin, nothing, ((0, 0, 0), (0, PAD, 0)))
    twin += lax.pad(mask_twin.astype(BF16), nothing, rest)
    held = jnp.where(away_carried & 1 == 0, mine, twin)

    bits = [1 << i for i in range(1, blocks.bit_length() - 1)]
    last = bits.pop()
    near, far = crossing(held, last)
    other = exchange(mine, 1, "section")
    same = away_wanted & last == 0
    far, near = lax.optimization_barrier((far, near))
    held = jnp.where(core == section, jnp.where(same, held, near), jnp.where(same, near, far))

    white = masks = None
    while bits:
        flips, bits = bits[:2], bits[2:]
        shifts = [flips[0] * k for k in range(1, 1 << len(flips))]
        got = [exchange(held, k) for k in shifts]
        if white is None:
            white, masks, *tables = call(
                receivers,
                [shaped(SEGS * ST, 2 * NF), shaped(SEGS * ST, LANES, dtype=F32)]
                + [shaped(*t.shape) for t in tables],
                [VMEM] * 2 + [HBM] * len(tables),
                [mine, other, *tables],
                [pltpu.SemaphoreType.DMA((len(tables),))],
                flops=10**9,
            )
            *got, white, masks = lax.optimization_barrier((*got, white, masks))
        rel = away_wanted & sum(flips)
        for k, piece in zip(shifts, got):
            held = jnp.where(rel == k, piece, held)
    twin = exchange(held, 1)
    return call(
        correlate,
        shaped(ST, ST, LAGS, dtype=F32),
        [VMEM] * 10,
        [held, twin, white, masks, *tables],
        flops=10**9,
        fused=[True] + [False] * 9,
    )


def solution(mesh):
    return jax.shard_map(
        shards,
        mesh=mesh,
        in_specs=(P("blk", "section"), P("blk", "section"), P()),
        out_specs=P("section", "blk", None),
        check_vma=False,
    )
```

```python
import math

import jax
import jax.numpy as jnp
import numpy as np
from jax import lax
from jax.experimental import pallas as pl
from jax.experimental.pallas import tpu as pltpu
from jax.sharding import PartitionSpec as P

L = 1024
NF = 384
BIN_LO = 8
LAGS = 256
TAPS = 33
HW = 50
WF = 32
ST = 8
SEGS = 8
BLK = 256
ROWS = SEGS * L // BLK
PAD = 128
LANES = 128

F32 = jnp.float32
BF16 = jnp.bfloat16


def halves(table):
    high = table.astype(BF16)
    low = (table - high.astype(np.float64)).astype(BF16)
    return high, low


def band(values):
    reach = len(values) // 2
    shift = LANES + np.arange(LANES)[None, :] - np.arange(3 * LANES)[:, None] + reach
    inside = (shift >= 0) & (shift < len(values))
    return np.where(inside, values[np.clip(shift, 0, len(values) - 1)], 0.0)


def filter_table():
    k = np.arange(TAPS, dtype=np.float64) - (TAPS - 1) // 2
    low, high = BIN_LO / L, (BIN_LO + NF) / L
    window = 0.5 + 0.5 * np.cos(2.0 * math.pi * k / (TAPS + 1))
    taps = window * (2 * high * np.sinc(2 * high * k) - 2 * low * np.sinc(2 * low * k))
    return np.concatenate(halves(band(taps)), axis=1)


def mean_table():
    return band(np.ones(2 * HW + 1)).astype(BF16)


def smooth_table():
    return band(np.ones(2 * WF + 1)).astype(BF16)


def forward_table():
    phase = np.mod(np.arange(BLK)[:, None] * (BIN_LO + np.arange(NF))[None, :], L) * (2.0 * math.pi / L)
    return np.concatenate([np.cos(phase), -np.sin(phase)], axis=1).astype(BF16)


def lag_table():
    shifts = np.arange(LAGS // 2)[None, :]
    phase = np.mod((BIN_LO + np.arange(NF))[:, None] * shifts, L) * (2.0 * math.pi / L)
    table = np.concatenate([np.cos(phase), -np.sin(phase)], axis=0) / math.sqrt(NF)
    return halves(table)


def dot(a, b):
    return jnp.dot(a, b, preferred_element_type=F32)


def split(a):
    high = a.astype(BF16)
    return high, (a - high.astype(F32)).astype(BF16)


def spread(parts):
    rows = []
    for part in parts:
        half = part.shape[1] - PAD
        rows += [part[:, i * BLK : (i + 1) * BLK].astype(F32) for i in range(half // BLK)]
    return rows


def mask_rows(parts):
    per = (parts[0].shape[1] - PAD) // L
    return jnp.concatenate([p[:, p.shape[1] - PAD :].astype(F32)[:per] for p in parts], axis=0)


def mask_column(mask):
    diagonal = lax.broadcasted_iota(jnp.int32, (ST, LANES), 0) == lax.broadcasted_iota(
        jnp.int32, (ST, LANES), 1
    )
    tiles = [jnp.where(diagonal, mask[g : g + 1], 0.0) for g in range(SEGS)]
    return jnp.sum(jnp.concatenate(tiles, axis=0), axis=1, keepdims=True)


def quarters(parts):
    parts = parts.reshape(SEGS, L // BLK, ST, 2 * NF)
    q0, q1, q2, q3 = (parts[:, q].reshape(SEGS * ST, 2 * NF) for q in range(L // BLK))
    turn = (BIN_LO + lax.broadcasted_iota(jnp.int32, (1, 2 * NF), 1)) % 4
    even = turn % 2 == 0
    here = jnp.where(even, q0 + q2, q0 - q2)
    there = jnp.where(even, q1 + q3, q1 - q3)
    there = jnp.where(turn >= 2, -there, there)
    real, imag = there[:, :NF], there[:, NF:]
    even = even[:, :NF]
    return here[:, :NF] + jnp.where(even, real, imag), here[:, NF:] + jnp.where(even, imag, -real)


def whitened(parts, column, table):
    zero = jnp.zeros((2 * ST, BLK), F32)
    x = jnp.concatenate([zero, *spread(parts), zero], axis=0)
    n = x.shape[0]
    half = BLK // 2
    window = jnp.concatenate(
        [x[: n - 2 * ST, half:], x[ST : n - ST], x[2 * ST :, :half]], axis=1
    ).astype(BF16)
    taps = table(0)
    columns = []
    for i in range(2):
        both = dot(window[:, i * half : i * half + 3 * half], taps)
        columns.append(both[:, :half] + both[:, half:])
    filtered = jnp.concatenate(columns, axis=1)
    m = filtered.shape[0]
    size = jnp.abs(filtered)
    window = jnp.concatenate(
        [size[: m - 2 * ST, half:], size[ST : m - ST], size[2 * ST :, :half]], axis=1
    )
    high, low = split(window)
    mean, zero = table(1), jnp.zeros((half, half), BF16)
    mean = jnp.concatenate(
        [jnp.concatenate([mean, zero], axis=0), jnp.concatenate([zero, mean], axis=0)], axis=1
    )
    total = dot(high, mean) + dot(low, mean)
    normal = filtered[ST : m - ST] / (total * (1.0 / (2 * HW + 1)) + 1e-06)
    real, imag = quarters(dot(normal.astype(BF16), table(3)))
    amplitude = jnp.sqrt(real * real + imag * imag)
    high, low = split(amplitude)
    smooth = table(2)
    zero = jnp.zeros((half, half), BF16)
    smooth = jnp.concatenate(
        [
            jnp.concatenate([smooth[half:], zero], axis=0),
            smooth,
            jnp.concatenate([zero, smooth[: 2 * half]], axis=0),
        ],
        axis=1,
    )
    both = dot(jnp.concatenate([high, low], axis=0), smooth)
    smoothed = both[: SEGS * ST] + both[SEGS * ST :]
    factor = column / (smoothed * (1.0 / (2 * WF + 1)) + 1e-06)
    return jnp.concatenate([real * factor, imag * factor], axis=1).astype(BF16)


def pack(raw, mask, order, mine, wanted, carried, order_here, mask_here, sems):
    half = raw.shape[1]
    ends = [(order, order_here), (mask, mask_here), (raw, mine.at[:, pl.ds(0, half)])]
    copies = [pltpu.make_async_copy(a, b, sems.at[i]) for i, (a, b) in enumerate(ends)]
    for copy in copies:
        copy.start()
    mine[:, half:] = jnp.zeros((ST, PAD), BF16)
    me = lax.axis_index("blk")
    copies[0].wait()
    for away, source in ((wanted, lax.axis_index("section")), (carried, me & 1)):
        away[...] = jnp.full(away.shape, order_here[source] ^ me, jnp.int32)
    copies[1].wait()
    segs, stations = mask.shape
    mine[:segs, half : half + stations] = mask_here[...].astype(F32).astype(BF16)
    copies[2].wait()


def ordered(swap, one, two):
    one, two = one[...], two[...]
    return jnp.where(swap == 0, one, two), jnp.where(swap == 0, two, one)


def receivers(mine, other, *refs):
    tables, (white, masks), held, sems = refs[:6], refs[6:8], refs[8:14], refs[14]
    copies = [pltpu.make_async_copy(a, b, sems.at[i]) for i, (a, b) in enumerate(zip(tables, held))]
    for copy in copies:
        copy.start()

    def table(i):
        copies[i].wait()
        return held[i][...]

    parts = ordered(lax.axis_index("section"), mine, other)
    column = mask_column(mask_rows(parts))
    masks[...] = jnp.broadcast_to(column, masks.shape)
    white[...] = whitened(parts, column, table)
    for copy in copies[4:]:
        copy.wait()


def correlate(held, twin, white, masks, *refs):
    tables, out = refs[:-1], refs[-1]
    parts = ordered(lax.axis_index("blk") & 1, held, twin)
    sent_mask = mask_rows(parts)
    column = mask_column(sent_mask)
    sent = whitened(parts, column, lambda i: tables[i][...]).astype(F32)
    lag_high, lag_low = tables[4:]
    recv = white[...].astype(F32)
    size = SEGS * ST
    common = sum(masks[g * ST : (g + 1) * ST] * sent_mask[g : g + 1] for g in range(SEGS))
    rows, counts = [], []
    for n in range(ST):
        real = jnp.zeros((ST, NF), F32)
        imag = jnp.zeros((ST, NF), F32)
        for g in range(SEGS):
            line = sent[g * ST + n : g * ST + n + 1]
            tile = recv[g * ST : (g + 1) * ST]
            sr, si = line[:, :NF], line[:, NF:]
            rr, ri = tile[:, :NF], tile[:, NF:]
            real += rr * sr + ri * si
            imag += ri * sr - rr * si
        rows.append(jnp.concatenate([real, imag], axis=1))
        counts.append(common[:, n : n + 1])
    stack = jnp.concatenate(rows, axis=0)
    bins = lax.broadcasted_iota(jnp.int32, (1, NF), 1) % 8
    cos = sum(jnp.where(bins == i, math.cos(math.pi * i / 4), 0.0) for i in range(8))
    sin = sum(jnp.where(bins == i, math.sin(math.pi * i / 4), 0.0) for i in range(8))
    real, imag = stack[:, :NF], stack[:, NF:]
    turned = jnp.concatenate([real * cos + imag * sin, imag * cos - real * sin], axis=1)
    high, low = split(jnp.concatenate([turned, stack], axis=0))
    both = dot(jnp.concatenate([high, low], axis=0), lag_high[...])
    lagged = both[: 2 * size] + both[2 * size :] + dot(high, lag_low[...])
    lagged = jnp.concatenate([lagged[:size], lagged[size:]], axis=1)
    lagged = lagged / jnp.maximum(jnp.concatenate(counts, axis=0), 1.0)
    out[...] = lagged.reshape(ST, ST, LAGS)


VMEM = pl.BlockSpec(memory_space=pltpu.VMEM)
HBM = pl.BlockSpec(memory_space=pltpu.HBM)


def call(body, out_shape, in_specs, arrays, scratch=(), flops=0):
    size = sum(a.size * a.dtype.itemsize for a in arrays)
    arrays = [
        pltpu.with_memory_space_constraint(a, pltpu.HBM) if spec is HBM else a
        for a, spec in zip(arrays, in_specs)
    ]
    return pl.pallas_call(
        body,
        out_shape=out_shape,
        in_specs=in_specs,
        out_specs=jax.tree.map(lambda _: VMEM, out_shape),
        scratch_shapes=scratch,
        cost_estimate=pl.CostEstimate(flops=flops, bytes_accessed=size, transcendentals=0),
        compiler_params=pltpu.CompilerParams(vmem_limit_bytes=16 * 1024 * 1024),
    )(*arrays)


def shaped(*shape, dtype=BF16):
    return jax.ShapeDtypeStruct(shape, dtype)


def exchange(x, flip, axis="blk"):
    devices = lax.axis_size(axis)
    return lax.ppermute(x, axis, [(i, i ^ flip) for i in range(devices)])


def exchange_by_class(x, one, two):
    blocks = lax.axis_size("blk")
    pairs = [
        (s * blocks + b, s * blocks + (b ^ (one if s == b % 2 else two)))
        for s in range(2)
        for b in range(blocks)
    ]
    return lax.ppermute(x, ("section", "blk"), pairs)


def crossing(x, bit):
    axes = ("section", "blk")
    blocks = lax.axis_size("blk")
    near, far = [], []
    for s in range(2):
        for b in range(blocks):
            here, there = s * blocks, (1 - s) * blocks
            if s == b % 2:
                near.append((here + b, here + (b ^ bit)))
                far.append((here + b, there + (b ^ 1)))
            else:
                near.append((here + b, there + (b ^ 1)))
                far.append((here + b, there + (b ^ 1 ^ bit)))
    return lax.ppermute(x, axes, near), lax.ppermute(x, axes, far)


def shards(raw_traces, valid_mask, block_order):
    section = lax.axis_index("section")
    blocks = lax.axis_size("blk")
    core = lax.axis_index("blk") & 1
    half = raw_traces.shape[1]
    width = half + PAD
    tables = [filter_table(), mean_table(), smooth_table(), forward_table(), *lag_table()]
    tables = [jnp.asarray(t) for t in tables]
    mine, away_wanted, away_carried = call(
        pack,
        [shaped(ST, width)] + [shaped(ST, width, dtype=jnp.int32)] * 2,
        [HBM] * 3,
        [raw_traces, valid_mask.T, block_order],
        [
            pltpu.SMEM(block_order.shape, jnp.int32),
            pltpu.VMEM(valid_mask.shape[::-1], jnp.int32),
            pltpu.SemaphoreType.DMA((3,)),
        ],
    )

    raw_twin, mask_twin, mine, away_wanted, away_carried = lax.optimization_barrier(
        (exchange(raw_traces, 1), exchange(valid_mask.T, 1), mine, away_wanted, away_carried)
    )
    nothing = jnp.zeros((), BF16)
    rest = ((0, ST - valid_mask.shape[1], 0), (half, PAD - ST, 0))
    twin = lax.pad(raw_twin, nothing, ((0, 0, 0), (0, PAD, 0)))
    twin += lax.pad(mask_twin.astype(BF16), nothing, rest)
    held = jnp.where(away_carried & 1 == 0, mine, twin)

    bits = [1 << i for i in range(1, blocks.bit_length() - 1)]
    last = bits.pop()
    near, far = crossing(held, last)
    other = exchange(mine, 1, "section")
    same = away_wanted & last == 0
    far, near = lax.optimization_barrier((far, near))
    held = jnp.where(core == section, jnp.where(same, held, near), jnp.where(same, near, far))

    white = masks = None
    while bits:
        flips, bits = bits[:2], bits[2:]
        shifts = [flips[0] * k for k in range(1, 1 << len(flips))]
        turned = [*shifts[:2][::-1], *shifts[2:]]
        got = [exchange_by_class(held, *k) for k in zip(shifts, turned)]
        if white is None:
            white, masks, *tables = call(
                receivers,
                [shaped(SEGS * ST, 2 * NF), shaped(SEGS * ST, LANES, dtype=F32)]
                + [shaped(*t.shape) for t in tables],
                [VMEM] * 2 + [HBM] * len(tables),
                [mine, other, *tables],
                [pltpu.SemaphoreType.DMA((len(tables),))],
                flops=10**9,
            )
            *got, white, masks = lax.optimization_barrier((*got, white, masks))
        rel = away_wanted & sum(flips)
        one = two = held
        for k, m, piece in zip(shifts, turned, got):
            one, two = jnp.where(rel == k, piece, one), jnp.where(rel == m, piece, two)
        held = jnp.where(core == section, one, two)
    twin = exchange(held, 1)
    return call(
        correlate,
        shaped(ST, ST, LAGS, dtype=F32),
        [VMEM] * 10,
        [held, twin, white, masks, *tables],
        flops=10**9,
    )


def solution(mesh):
    return jax.shard_map(
        shards,
        mesh=mesh,
        in_specs=(P("blk", "section"), P("blk", "section"), P()),
        out_specs=P("section", "blk", None),
        check_vma=False,
    )
```

```python
import math

import jax
import jax.numpy as jnp
import numpy as np
from jax import lax
from jax.experimental import pallas as pl
from jax.experimental.pallas import tpu as pltpu
from jax.sharding import PartitionSpec as P

L = 1024
NF = 384
BIN_LO = 8
LAGS = 256
TAPS = 33
HW = 50
WF = 32
ST = 8
SEGS = 8
BLK = 256
ROWS = SEGS * L // BLK
PAD = 128
LANES = 128

F32 = jnp.float32
BF16 = jnp.bfloat16


def halves(table):
    high = table.astype(BF16)
    low = (table - high.astype(np.float64)).astype(BF16)
    return high, low


def band(values):
    reach = len(values) // 2
    shift = LANES + np.arange(LANES)[None, :] - np.arange(3 * LANES)[:, None] + reach
    inside = (shift >= 0) & (shift < len(values))
    return np.where(inside, values[np.clip(shift, 0, len(values) - 1)], 0.0)


def filter_table():
    k = np.arange(TAPS, dtype=np.float64) - (TAPS - 1) // 2
    low, high = BIN_LO / L, (BIN_LO + NF) / L
    window = 0.5 + 0.5 * np.cos(2.0 * math.pi * k / (TAPS + 1))
    taps = window * (2 * high * np.sinc(2 * high * k) - 2 * low * np.sinc(2 * low * k))
    return np.concatenate(halves(band(taps)), axis=1)


def mean_table():
    return band(np.ones(2 * HW + 1)).astype(BF16)


def smooth_table():
    return band(np.ones(2 * WF + 1)).astype(BF16)


def forward_table():
    phase = np.mod(np.arange(BLK)[:, None] * (BIN_LO + np.arange(NF))[None, :], L) * (2.0 * math.pi / L)
    return np.concatenate([np.cos(phase), -np.sin(phase)], axis=1).astype(BF16)


def lag_table():
    shifts = np.arange(LAGS // 2)[None, :]
    phase = np.mod((BIN_LO + np.arange(NF))[:, None] * shifts, L) * (2.0 * math.pi / L)
    table = np.concatenate([np.cos(phase), -np.sin(phase)], axis=0) / math.sqrt(NF)
    return halves(table)


def dot(a, b):
    return jnp.dot(a, b, preferred_element_type=F32)


def split(a):
    high = a.astype(BF16)
    return high, (a - high.astype(F32)).astype(BF16)


def spread(parts):
    rows = []
    for part in parts:
        half = part.shape[1] - PAD
        rows += [part[:, i * BLK : (i + 1) * BLK].astype(F32) for i in range(half // BLK)]
    return rows


def mask_rows(parts):
    per = (parts[0].shape[1] - PAD) // L
    return jnp.concatenate([p[:, p.shape[1] - PAD :].astype(F32)[:per] for p in parts], axis=0)


def mask_column(mask):
    diagonal = lax.broadcasted_iota(jnp.int32, (ST, LANES), 0) == lax.broadcasted_iota(
        jnp.int32, (ST, LANES), 1
    )
    tiles = [jnp.where(diagonal, mask[g : g + 1], 0.0) for g in range(SEGS)]
    return jnp.sum(jnp.concatenate(tiles, axis=0), axis=1, keepdims=True)


def quarters(parts):
    parts = parts.reshape(SEGS, L // BLK, ST, 2 * NF)
    q0, q1, q2, q3 = (parts[:, q].reshape(SEGS * ST, 2 * NF) for q in range(L // BLK))
    turn = (BIN_LO + lax.broadcasted_iota(jnp.int32, (1, 2 * NF), 1)) % 4
    even = turn % 2 == 0
    here = jnp.where(even, q0 + q2, q0 - q2)
    there = jnp.where(even, q1 + q3, q1 - q3)
    there = jnp.where(turn >= 2, -there, there)
    real, imag = there[:, :NF], there[:, NF:]
    even = even[:, :NF]
    return here[:, :NF] + jnp.where(even, real, imag), here[:, NF:] + jnp.where(even, imag, -real)


def whitened(parts, column, table):
    zero = jnp.zeros((2 * ST, BLK), F32)
    x = jnp.concatenate([zero, *spread(parts), zero], axis=0)
    n = x.shape[0]
    half = BLK // 2
    window = jnp.concatenate(
        [x[: n - 2 * ST, half:], x[ST : n - ST], x[2 * ST :, :half]], axis=1
    ).astype(BF16)
    taps = table(0)
    columns = []
    for i in range(2):
        both = dot(window[:, i * half : i * half + 3 * half], taps)
        columns.append(both[:, :half] + both[:, half:])
    filtered = jnp.concatenate(columns, axis=1)
    m = filtered.shape[0]
    size = jnp.abs(filtered)
    window = jnp.concatenate(
        [size[: m - 2 * ST, half:], size[ST : m - ST], size[2 * ST :, :half]], axis=1
    )
    high, low = split(window)
    mean, zero = table(1), jnp.zeros((half, half), BF16)
    mean = jnp.concatenate(
        [jnp.concatenate([mean, zero], axis=0), jnp.concatenate([zero, mean], axis=0)], axis=1
    )
    total = dot(high, mean) + dot(low, mean)
    normal = filtered[ST : m - ST] / (total * (1.0 / (2 * HW + 1)) + 1e-06)
    real, imag = quarters(dot(normal.astype(BF16), table(3)))
    amplitude = jnp.sqrt(real * real + imag * imag)
    high, low = split(amplitude)
    smooth = table(2)
    zero = jnp.zeros((half, half), BF16)
    smooth = jnp.concatenate(
        [
            jnp.concatenate([smooth[half:], zero], axis=0),
            smooth,
            jnp.concatenate([zero, smooth[: 2 * half]], axis=0),
        ],
        axis=1,
    )
    both = dot(jnp.concatenate([high, low], axis=0), smooth)
    smoothed = both[: SEGS * ST] + both[SEGS * ST :]
    factor = column / (smoothed * (1.0 / (2 * WF + 1)) + 1e-06)
    return jnp.concatenate([real * factor, imag * factor], axis=1).astype(BF16)


def pack(raw, mask, order, mine, wanted, carried, order_here, mask_here, sems):
    half = raw.shape[1]
    ends = [(order, order_here), (mask, mask_here), (raw, mine.at[:, pl.ds(0, half)])]
    copies = [pltpu.make_async_copy(a, b, sems.at[i]) for i, (a, b) in enumerate(ends)]
    for copy in copies:
        copy.start()
    mine[:, half:] = jnp.zeros((ST, PAD), BF16)
    me = lax.axis_index("blk")
    copies[0].wait()
    for away, source in ((wanted, lax.axis_index("section")), (carried, me & 1)):
        away[...] = jnp.full(away.shape, order_here[source] ^ me, jnp.int32)
    copies[1].wait()
    segs, stations = mask.shape
    mine[:segs, half : half + stations] = mask_here[...].astype(F32).astype(BF16)
    copies[2].wait()


def ordered(swap, one, two):
    one, two = one[...], two[...]
    return jnp.where(swap == 0, one, two), jnp.where(swap == 0, two, one)


def receivers(mine, other, *refs):
    tables, (white, masks), held, sems = refs[:6], refs[6:8], refs[8:14], refs[14]
    copies = [pltpu.make_async_copy(a, b, sems.at[i]) for i, (a, b) in enumerate(zip(tables, held))]
    for copy in copies:
        copy.start()

    def table(i):
        copies[i].wait()
        return held[i][...]

    parts = ordered(lax.axis_index("section"), mine, other)
    column = mask_column(mask_rows(parts))
    masks[...] = jnp.broadcast_to(column, masks.shape)
    white[...] = whitened(parts, column, table)
    for copy in copies[4:]:
        copy.wait()


def correlate(held, twin, white, masks, *refs):
    tables, out = refs[:-1], refs[-1]
    parts = ordered(lax.axis_index("blk") & 1, held, twin)
    sent_mask = mask_rows(parts)
    column = mask_column(sent_mask)
    sent = whitened(parts, column, lambda i: tables[i][...]).astype(F32)
    lag_high, lag_low = tables[4:]
    recv = white[...].astype(F32)
    size = SEGS * ST
    common = sum(masks[g * ST : (g + 1) * ST] * sent_mask[g : g + 1] for g in range(SEGS))
    rows, counts = [], []
    for n in range(ST):
        real = jnp.zeros((ST, NF), F32)
        imag = jnp.zeros((ST, NF), F32)
        for g in range(SEGS):
            line = sent[g * ST + n : g * ST + n + 1]
            tile = recv[g * ST : (g + 1) * ST]
            sr, si = line[:, :NF], line[:, NF:]
            rr, ri = tile[:, :NF], tile[:, NF:]
            real += rr * sr + ri * si
            imag += ri * sr - rr * si
        rows.append(jnp.concatenate([real, imag], axis=1))
        counts.append(common[:, n : n + 1])
    stack = jnp.concatenate(rows, axis=0)
    bins = lax.broadcasted_iota(jnp.int32, (1, NF), 1) % 8
    cos = sum(jnp.where(bins == i, math.cos(math.pi * i / 4), 0.0) for i in range(8))
    sin = sum(jnp.where(bins == i, math.sin(math.pi * i / 4), 0.0) for i in range(8))
    real, imag = stack[:, :NF], stack[:, NF:]
    turned = jnp.concatenate([real * cos + imag * sin, imag * cos - real * sin], axis=1)
    high, low = split(jnp.concatenate([turned, stack], axis=0))
    both = dot(jnp.concatenate([high, low], axis=0), lag_high[...])
    lagged = both[: 2 * size] + both[2 * size :] + dot(high, lag_low[...])
    lagged = jnp.concatenate([lagged[:size], lagged[size:]], axis=1)
    lagged = lagged / jnp.maximum(jnp.concatenate(counts, axis=0), 1.0)
    out[...] = lagged.reshape(ST, ST, LAGS)


VMEM = pl.BlockSpec(memory_space=pltpu.VMEM)
HBM = pl.BlockSpec(memory_space=pltpu.HBM)


def call(body, out_shape, in_specs, arrays, scratch=(), flops=0, fused=None):
    size = sum(a.size * a.dtype.itemsize for a in arrays)
    arrays = [
        pltpu.with_memory_space_constraint(a, pltpu.HBM) if spec is HBM else a
        for a, spec in zip(arrays, in_specs)
    ]
    return pl.pallas_call(
        body,
        out_shape=out_shape,
        in_specs=in_specs,
        out_specs=jax.tree.map(lambda _: VMEM, out_shape),
        scratch_shapes=scratch,
        cost_estimate=pl.CostEstimate(flops=flops, bytes_accessed=size, transcendentals=0),
        compiler_params=pltpu.CompilerParams(vmem_limit_bytes=16 * 1024 * 1024, allow_input_fusion=fused),
    )(*arrays)


def shaped(*shape, dtype=BF16):
    return jax.ShapeDtypeStruct(shape, dtype)


def exchange(x, flip, axis="blk"):
    devices = lax.axis_size(axis)
    return lax.ppermute(x, axis, [(i, i ^ flip) for i in range(devices)])


def exchange_by_class(x, one, two):
    blocks = lax.axis_size("blk")
    pairs = [
        (s * blocks + b, s * blocks + (b ^ (one if s == b % 2 else two)))
        for s in range(2)
        for b in range(blocks)
    ]
    return lax.ppermute(x, ("section", "blk"), pairs)


def crossing(x, bit):
    axes = ("section", "blk")
    blocks = lax.axis_size("blk")
    near, far = [], []
    for s in range(2):
        for b in range(blocks):
            here, there = s * blocks, (1 - s) * blocks
            if s == b % 2:
                near.append((here + b, here + (b ^ bit)))
                far.append((here + b, there + (b ^ 1)))
            else:
                near.append((here + b, there + (b ^ 1)))
                far.append((here + b, there + (b ^ 1 ^ bit)))
    return lax.ppermute(x, axes, near), lax.ppermute(x, axes, far)


def shards(raw_traces, valid_mask, block_order):
    section = lax.axis_index("section")
    blocks = lax.axis_size("blk")
    core = lax.axis_index("blk") & 1
    half = raw_traces.shape[1]
    width = half + PAD
    tables = [filter_table(), mean_table(), smooth_table(), forward_table(), *lag_table()]
    tables = [jnp.asarray(t) for t in tables]
    mine, away_wanted, away_carried = call(
        pack,
        [shaped(ST, width)] + [shaped(ST, width, dtype=jnp.int32)] * 2,
        [HBM] * 3,
        [raw_traces, valid_mask.T, block_order],
        [
            pltpu.SMEM(block_order.shape, jnp.int32),
            pltpu.VMEM(valid_mask.shape[::-1], jnp.int32),
            pltpu.SemaphoreType.DMA((3,)),
        ],
    )

    raw_twin, mask_twin, mine, away_wanted, away_carried = lax.optimization_barrier(
        (exchange(raw_traces, 1), exchange(valid_mask.T, 1), mine, away_wanted, away_carried)
    )
    nothing = jnp.zeros((), BF16)
    rest = ((0, ST - valid_mask.shape[1], 0), (half, PAD - ST, 0))
    twin = lax.pad(raw_twin, nothing, ((0, 0, 0), (0, PAD, 0)))
    twin += lax.pad(mask_twin.astype(BF16), nothing, rest)
    held = jnp.where(away_carried & 1 == 0, mine, twin)

    bits = [1 << i for i in range(1, blocks.bit_length() - 1)]
    last = bits.pop()
    near, far = crossing(held, last)
    other = exchange(mine, 1, "section")
    same = away_wanted & last == 0
    far, near = lax.optimization_barrier((far, near))
    held = jnp.where(core == section, jnp.where(same, held, near), jnp.where(same, near, far))

    white = masks = None
    while bits:
        flips, bits = bits[:2], bits[2:]
        shifts = [flips[0] * k for k in range(1, 1 << len(flips))]
        turned = [*shifts[:2][::-1], *shifts[2:]]
        got = [exchange_by_class(held, *k) for k in zip(shifts, turned)]
        if white is None:
            white, masks, *tables = call(
                receivers,
                [shaped(SEGS * ST, 2 * NF), shaped(SEGS * ST, LANES, dtype=F32)]
                + [shaped(*t.shape) for t in tables],
                [VMEM] * 2 + [HBM] * len(tables),
                [mine, other, *tables],
                [pltpu.SemaphoreType.DMA((len(tables),))],
                flops=10**9,
            )
            *got, white, masks = lax.optimization_barrier((*got, white, masks))
        rel = away_wanted & sum(flips)
        one = two = held
        for k, m, piece in zip(shifts, turned, got):
            one, two = jnp.where(rel == k, piece, one), jnp.where(rel == m, piece, two)
        held = jnp.where(core == section, one, two)
    twin = exchange(held, 1)
    return call(
        correlate,
        shaped(ST, ST, LAGS, dtype=F32),
        [VMEM] * 10,
        [held, twin, white, masks, *tables],
        flops=10**9,
        fused=[True] + [False] * 9,
    )


def solution(mesh):
    return jax.shard_map(
        shards,
        mesh=mesh,
        in_specs=(P("blk", "section"), P("blk", "section"), P()),
        out_specs=P("section", "blk", None),
        check_vma=False,
    )
```

```python
import math

import jax
import jax.numpy as jnp
import numpy as np
from jax import lax
from jax.experimental import pallas as pl
from jax.experimental.pallas import tpu as pltpu
from jax.sharding import PartitionSpec as P

L = 1024
NF = 384
BIN_LO = 8
LAGS = 256
TAPS = 33
HW = 50
WF = 32
ST = 8
SEGS = 8
BLK = 256
ROWS = SEGS * L // BLK
PAD = 128
LANES = 128

F32 = jnp.float32
BF16 = jnp.bfloat16


def halves(table):
    high = table.astype(BF16)
    low = (table - high.astype(np.float64)).astype(BF16)
    return high, low


def band(values):
    reach = len(values) // 2
    shift = LANES + np.arange(LANES)[None, :] - np.arange(3 * LANES)[:, None] + reach
    inside = (shift >= 0) & (shift < len(values))
    return np.where(inside, values[np.clip(shift, 0, len(values) - 1)], 0.0)


def filter_table():
    k = np.arange(TAPS, dtype=np.float64) - (TAPS - 1) // 2
    low, high = BIN_LO / L, (BIN_LO + NF) / L
    window = 0.5 + 0.5 * np.cos(2.0 * math.pi * k / (TAPS + 1))
    taps = window * (2 * high * np.sinc(2 * high * k) - 2 * low * np.sinc(2 * low * k))
    return np.concatenate(halves(band(taps)), axis=1)


def mean_table():
    return band(np.ones(2 * HW + 1)).astype(BF16)


def smooth_table():
    return band(np.ones(2 * WF + 1)).astype(BF16)


def forward_table():
    phase = np.mod(np.arange(BLK)[:, None] * (BIN_LO + np.arange(NF))[None, :], L) * (2.0 * math.pi / L)
    return np.concatenate([np.cos(phase), -np.sin(phase)], axis=1).astype(BF16)


def lag_table():
    shifts = np.arange(LAGS // 2)[None, :]
    phase = np.mod((BIN_LO + np.arange(NF))[:, None] * shifts, L) * (2.0 * math.pi / L)
    table = np.concatenate([np.cos(phase), -np.sin(phase)], axis=0) / math.sqrt(NF)
    return halves(table)


def dot(a, b):
    return jnp.dot(a, b, preferred_element_type=F32)


def split(a):
    high = a.astype(BF16)
    return high, (a - high.astype(F32)).astype(BF16)


def spread(parts):
    rows = []
    for part in parts:
        half = part.shape[1] - PAD
        rows += [part[:, i * BLK : (i + 1) * BLK].astype(F32) for i in range(half // BLK)]
    return rows


def mask_rows(parts):
    per = (parts[0].shape[1] - PAD) // L
    return jnp.concatenate([p[:, p.shape[1] - PAD :].astype(F32)[:per] for p in parts], axis=0)


def mask_column(mask):
    diagonal = lax.broadcasted_iota(jnp.int32, (ST, LANES), 0) == lax.broadcasted_iota(
        jnp.int32, (ST, LANES), 1
    )
    tiles = [jnp.where(diagonal, mask[g : g + 1], 0.0) for g in range(SEGS)]
    return jnp.sum(jnp.concatenate(tiles, axis=0), axis=1, keepdims=True)


def quarters(parts):
    parts = parts.reshape(SEGS, L // BLK, ST, 2 * NF)
    q0, q1, q2, q3 = (parts[:, q].reshape(SEGS * ST, 2 * NF) for q in range(L // BLK))
    turn = (BIN_LO + lax.broadcasted_iota(jnp.int32, (1, 2 * NF), 1)) % 4
    even = turn % 2 == 0
    here = jnp.where(even, q0 + q2, q0 - q2)
    there = jnp.where(even, q1 + q3, q1 - q3)
    there = jnp.where(turn >= 2, -there, there)
    real, imag = there[:, :NF], there[:, NF:]
    even = even[:, :NF]
    return here[:, :NF] + jnp.where(even, real, imag), here[:, NF:] + jnp.where(even, imag, -real)


def whitened(parts, column, table):
    zero = jnp.zeros((2 * ST, BLK), F32)
    x = jnp.concatenate([zero, *spread(parts), zero], axis=0)
    n = x.shape[0]
    half = BLK // 2
    window = jnp.concatenate(
        [x[: n - 2 * ST, half:], x[ST : n - ST], x[2 * ST :, :half]], axis=1
    ).astype(BF16)
    taps = table(0)
    columns = []
    for i in range(2):
        both = dot(window[:, i * half : i * half + 3 * half], taps)
        columns.append(both[:, :half] + both[:, half:])
    filtered = jnp.concatenate(columns, axis=1)
    m = filtered.shape[0]
    size = jnp.abs(filtered)
    window = jnp.concatenate(
        [size[: m - 2 * ST, half:], size[ST : m - ST], size[2 * ST :, :half]], axis=1
    )
    high, low = split(window)
    mean, zero = table(1), jnp.zeros((half, half), BF16)
    mean = jnp.concatenate(
        [jnp.concatenate([mean, zero], axis=0), jnp.concatenate([zero, mean], axis=0)], axis=1
    )
    total = dot(high, mean) + dot(low, mean)
    normal = filtered[ST : m - ST] / (total * (1.0 / (2 * HW + 1)) + 1e-06)
    real, imag = quarters(dot(normal.astype(BF16), table(3)))
    amplitude = jnp.sqrt(real * real + imag * imag)
    high, low = split(amplitude)
    smooth = table(2)
    zero = jnp.zeros((half, half), BF16)
    smooth = jnp.concatenate(
        [
            jnp.concatenate([smooth[half:], zero], axis=0),
            smooth,
            jnp.concatenate([zero, smooth[: 2 * half]], axis=0),
        ],
        axis=1,
    )
    both = dot(jnp.concatenate([high, low], axis=0), smooth)
    smoothed = both[: SEGS * ST] + both[SEGS * ST :]
    factor = column / (smoothed * (1.0 / (2 * WF + 1)) + 1e-06)
    return jnp.concatenate([real * factor, imag * factor], axis=1).astype(BF16)


def pack(raw, mask, order, mine, wanted, carried, order_here, mask_here, sems):
    half = raw.shape[1]
    ends = [(order, order_here), (mask, mask_here), (raw, mine.at[:, pl.ds(0, half)])]
    copies = [pltpu.make_async_copy(a, b, sems.at[i]) for i, (a, b) in enumerate(ends)]
    for copy in copies:
        copy.start()
    mine[:, half:] = jnp.zeros((ST, PAD), BF16)
    me = lax.axis_index("blk")
    copies[0].wait()
    for away, source in ((wanted, lax.axis_index("section")), (carried, me & 1)):
        away[...] = jnp.full(away.shape, order_here[source] ^ me, jnp.int32)
    copies[1].wait()
    segs, stations = mask.shape
    mine[:segs, half : half + stations] = mask_here[...].astype(F32).astype(BF16)
    copies[2].wait()


def ordered(swap, one, two):
    one, two = one[...], two[...]
    return jnp.where(swap == 0, one, two), jnp.where(swap == 0, two, one)


def receivers(mine, other, *refs):
    tables, (white, masks), held, sems = refs[:6], refs[6:8], refs[8:14], refs[14]
    copies = [pltpu.make_async_copy(a, b, sems.at[i]) for i, (a, b) in enumerate(zip(tables, held))]
    for copy in copies:
        copy.start()

    def table(i):
        copies[i].wait()
        return held[i][...]

    parts = ordered(lax.axis_index("section"), mine, other)
    column = mask_column(mask_rows(parts))
    masks[...] = jnp.broadcast_to(column, masks.shape)
    white[...] = whitened(parts, column, table)
    for copy in copies[4:]:
        copy.wait()


def correlate(held, twin, white, masks, *refs):
    tables, out = refs[:-1], refs[-1]
    parts = ordered(lax.axis_index("blk") & 1, held, twin)
    sent_mask = mask_rows(parts)
    column = mask_column(sent_mask)
    sent = whitened(parts, column, lambda i: tables[i][...]).astype(F32)
    lag_high, lag_low = tables[4:]
    recv = white[...].astype(F32)
    size = SEGS * ST
    common = sum(masks[g * ST : (g + 1) * ST] * sent_mask[g : g + 1] for g in range(SEGS))
    rows, counts = [], []
    for n in range(ST):
        real = jnp.zeros((ST, NF), F32)
        imag = jnp.zeros((ST, NF), F32)
        for g in range(SEGS):
            line = sent[g * ST + n : g * ST + n + 1]
            tile = recv[g * ST : (g + 1) * ST]
            sr, si = line[:, :NF], line[:, NF:]
            rr, ri = tile[:, :NF], tile[:, NF:]
            real += rr * sr + ri * si
            imag += ri * sr - rr * si
        rows.append(jnp.concatenate([real, imag], axis=1))
        counts.append(common[:, n : n + 1])
    stack = jnp.concatenate(rows, axis=0)
    bins = lax.broadcasted_iota(jnp.int32, (1, NF), 1) % 8
    cos = sum(jnp.where(bins == i, math.cos(math.pi * i / 4), 0.0) for i in range(8))
    sin = sum(jnp.where(bins == i, math.sin(math.pi * i / 4), 0.0) for i in range(8))
    real, imag = stack[:, :NF], stack[:, NF:]
    turned = jnp.concatenate([real * cos + imag * sin, imag * cos - real * sin], axis=1)
    high, low = split(jnp.concatenate([turned, stack], axis=0))
    both = dot(jnp.concatenate([high, low], axis=0), lag_high[...])
    lagged = both[: 2 * size] + both[2 * size :] + dot(high, lag_low[...])
    lagged = jnp.concatenate([lagged[:size], lagged[size:]], axis=1)
    lagged = lagged * (1.0 / jnp.maximum(jnp.concatenate(counts, axis=0), 1.0))
    out[...] = lagged.reshape(ST, ST, LAGS)


VMEM = pl.BlockSpec(memory_space=pltpu.VMEM)
HBM = pl.BlockSpec(memory_space=pltpu.HBM)


def call(body, out_shape, in_specs, arrays, scratch=(), flops=0):
    size = sum(a.size * a.dtype.itemsize for a in arrays)
    arrays = [
        pltpu.with_memory_space_constraint(a, pltpu.HBM) if spec is HBM else a
        for a, spec in zip(arrays, in_specs)
    ]
    return pl.pallas_call(
        body,
        out_shape=out_shape,
        in_specs=in_specs,
        out_specs=jax.tree.map(lambda _: VMEM, out_shape),
        scratch_shapes=scratch,
        cost_estimate=pl.CostEstimate(flops=flops, bytes_accessed=size, transcendentals=0),
        compiler_params=pltpu.CompilerParams(vmem_limit_bytes=16 * 1024 * 1024),
    )(*arrays)


def shaped(*shape, dtype=BF16):
    return jax.ShapeDtypeStruct(shape, dtype)


def exchange(x, flip, axis="blk"):
    devices = lax.axis_size(axis)
    return lax.ppermute(x, axis, [(i, i ^ flip) for i in range(devices)])


def crossing(x, bit):
    axes = ("section", "blk")
    blocks = lax.axis_size("blk")
    near, far = [], []
    for s in range(2):
        for b in range(blocks):
            here, there = s * blocks, (1 - s) * blocks
            if s == b % 2:
                near.append((here + b, here + (b ^ bit)))
                far.append((here + b, there + (b ^ 1)))
            else:
                near.append((here + b, there + (b ^ 1)))
                far.append((here + b, there + (b ^ 1 ^ bit)))
    return lax.ppermute(x, axes, near), lax.ppermute(x, axes, far)


def shards(raw_traces, valid_mask, block_order):
    section = lax.axis_index("section")
    blocks = lax.axis_size("blk")
    core = lax.axis_index("blk") & 1
    half = raw_traces.shape[1]
    width = half + PAD
    tables = [filter_table(), mean_table(), smooth_table(), forward_table(), *lag_table()]
    tables = [jnp.asarray(t) for t in tables]
    mine, away_wanted, away_carried = call(
        pack,
        [shaped(ST, width)] + [shaped(ST, width, dtype=jnp.int32)] * 2,
        [HBM] * 3,
        [raw_traces, valid_mask.T, block_order],
        [
            pltpu.SMEM(block_order.shape, jnp.int32),
            pltpu.VMEM(valid_mask.shape[::-1], jnp.int32),
            pltpu.SemaphoreType.DMA((3,)),
        ],
    )

    raw_twin, mask_twin, mine, away_wanted, away_carried = lax.optimization_barrier(
        (exchange(raw_traces, 1), exchange(valid_mask.T, 1), mine, away_wanted, away_carried)
    )
    nothing = jnp.zeros((), BF16)
    rest = ((0, ST - valid_mask.shape[1], 0), (half, PAD - ST, 0))
    twin = lax.pad(raw_twin, nothing, ((0, 0, 0), (0, PAD, 0)))
    twin += lax.pad(mask_twin.astype(BF16), nothing, rest)
    held = jnp.where(away_carried & 1 == 0, mine, twin)

    bits = [1 << i for i in range(1, blocks.bit_length() - 1)]
    last = bits.pop()
    near, far = crossing(held, last)
    other = exchange(mine, 1, "section")
    same = away_wanted & last == 0
    far, near = lax.optimization_barrier((far, near))
    held = jnp.where(core == section, jnp.where(same, held, near), jnp.where(same, near, far))

    white = masks = None
    while bits:
        flips, bits = bits[:2], bits[2:]
        shifts = [flips[0] * k for k in range(1, 1 << len(flips))]
        got = [exchange(held, k) for k in shifts]
        if white is None:
            white, masks, *tables = call(
                receivers,
                [shaped(SEGS * ST, 2 * NF), shaped(SEGS * ST, LANES, dtype=F32)]
                + [shaped(*t.shape) for t in tables],
                [VMEM] * 2 + [HBM] * len(tables),
                [mine, other, *tables],
                [pltpu.SemaphoreType.DMA((len(tables),))],
                flops=10**9,
            )
            *got, white, masks = lax.optimization_barrier((*got, white, masks))
        rel = away_wanted & sum(flips)
        for k, piece in zip(shifts, got):
            held = jnp.where(rel == k, piece, held)
    twin = exchange(held, 1)
    return call(
        correlate,
        shaped(ST, ST, LAGS, dtype=F32),
        [VMEM] * 10,
        [held, twin, white, masks, *tables],
        flops=10**9,
    )


def solution(mesh):
    return jax.shard_map(
        shards,
        mesh=mesh,
        in_specs=(P("blk", "section"), P("blk", "section"), P()),
        out_specs=P("section", "blk", None),
        check_vma=False,
    )
```
